32 devices in a mesh: pipe: 4 (over y, x), seq: 8 (over z, core).
Axes of the slice: x: 2, y: 2, z: 4, core: 2. Of those that a mesh axis runs over, the one named last changes fastest.
Arguments:
- acts: bfloat16 [4, 2048, 1024], P('pipe', 'seq'), may hold values from -6 to 6
- cotan: bfloat16 [4, 2048, 1024], P('pipe', 'seq'), may hold values from -6 to 6
- proj_in: bfloat16 [4, 1024, 2048], P('pipe'), may hold values from -0.1875 to 0.1875
- proj_out: bfloat16 [4, 1024, 1024], P('pipe'), may hold values from -0.1875 to 0.1875
- block_mix: bfloat16 [4, 2048, 256], P('pipe', 'seq'), may hold values from -0.375 to 0.375
- twiddle: float32 [4, 3, 2, 2, 1024], P('pipe'), may hold values from -2.5 to 2.5
Outputs:
- mixed: bfloat16 [4, 2048, 1024], P('pipe', 'seq')
- grad_prev: bfloat16 [4, 2048, 1024], P('pipe', 'seq')
- grad_in_proj: float32 [4, 1024, 2048], P('pipe', 'seq')
- grad_out_proj: float32 [4, 1024, 1024], P('pipe', 'seq')
- grad_block_mix: float32 [4, 2048, 256], P('pipe', 'seq')
- grad_twiddle: float32 [4, 3, 2, 2, 1024], P('pipe')
The draws below stay inside these ranges and needn't reach their ends.
All inputs are finite; a program needn't handle non-finite values.
Results may differ from the reference program's by a relative error of at most 0.014.
Values may be sent and summed in bfloat16 or wider, within the bound.
No kernel may reach another device: no remote copies, remote signals or barrier semaphores. Data moves between devices by JAX's collectives and lax.ppermute only.
A program may use at most 128 MiB of HBM per device.

```python
import jax
import jax.numpy as jnp

D = 1024
TOK_DEV = 256
SECTIONS = 4
LEN = 2048
BITS = 3
N_SEQ = 8


def levels(stream_key, extent, shards, smallest, top_value):
    loudness, own = 1.0, jax.random.fold_in(stream_key, 6)
    for axis_at, shards_of in shards:
        draws = jnp.exp(jax.random.uniform(jax.random.fold_in(own, axis_at), (shards_of,), jnp.float32, smallest / len(shards), top_value / len(shards)))
        loudness = loudness * jnp.repeat(draws, extent[axis_at] // shards_of).reshape([-1 if axis == axis_at else 1 for axis in range(len(extent))])
    return loudness


def normal_values(stream_key, shape, scale, reach, split=(), kind=jnp.bfloat16):
    drawn = jax.random.normal(stream_key, shape, jnp.float32) * scale
    if len(split) > 0:
        drawn = levels(stream_key, shape, split, -0.22, 0.18) * drawn
    return jnp.clip(drawn, min=-reach, max=reach).astype(kind)


def setup_inputs(seed: int = 0) -> dict:
    key_of = jax.random.split(jax.random.key(seed), 7)
    acts = normal_values(key_of[0], (SECTIONS, LEN, D), 1.0, 6.0, ((0, 4), (1, 8)))
    cotan = normal_values(key_of[1], (SECTIONS, LEN, D), 1.0, 6.0, ((0, 4), (1, 8)))
    proj_in = normal_values(key_of[2], (SECTIONS, D, 2 * D), D ** -0.5, 0.1875, ((0, 4),))
    proj_out = normal_values(key_of[3], (SECTIONS, D, D), D ** -0.5, 0.1875, ((0, 4),))
    block_mix = normal_values(key_of[4], (SECTIONS, LEN, TOK_DEV), TOK_DEV ** -0.5, 0.375, ((0, 4), (1, 8)))
    twiddle = normal_values(key_of[5], (SECTIONS, BITS, 2, 2, D), 0.7, 2.5, ((0, 4),), jnp.float32)
    return dict(acts=acts, cotan=cotan, proj_in=proj_in, proj_out=proj_out, block_mix=block_mix, twiddle=twiddle)


def local_segment(blocked, segment_coef, segment_bit):
    block_count, inner_rows, feature_count = blocked.shape
    stride_len = 2 ** segment_bit
    shaped = blocked.reshape(block_count // (2 * stride_len), 2, stride_len, inner_rows, feature_count)
    lower_part = shaped[:, 0].astype(jnp.float32)
    upper_part = shaped[:, 1].astype(jnp.float32)
    new_lower = segment_coef[0, 0] * lower_part + segment_coef[0, 1] * upper_part
    new_upper = segment_coef[1, 0] * upper_part + segment_coef[1, 1] * lower_part
    joined = jnp.stack([new_lower, new_upper], axis=1)
    return joined.reshape(block_count, inner_rows, feature_count).astype(jnp.bfloat16)


def local_back(grad_blocked, stored, segment_coef, segment_bit):
    block_count, inner_rows, feature_count = grad_blocked.shape
    stride_len = 2 ** segment_bit
    dshape = grad_blocked.reshape(block_count // (2 * stride_len), 2, stride_len, inner_rows, feature_count)
    zshape = stored.reshape(block_count // (2 * stride_len), 2, stride_len, inner_rows, feature_count)
    grad_lower = dshape[:, 0].astype(jnp.float32)
    grad_upper = dshape[:, 1].astype(jnp.float32)
    val_lower = zshape[:, 0].astype(jnp.float32)
    val_upper = zshape[:, 1].astype(jnp.float32)
    prev_lower = segment_coef[0, 0] * grad_lower + segment_coef[1, 1] * grad_upper
    prev_upper = segment_coef[1, 0] * grad_upper + segment_coef[0, 1] * grad_lower
    joined = jnp.stack([prev_lower, prev_upper], axis=1)
    prev = joined.reshape(block_count, inner_rows, feature_count).astype(jnp.bfloat16)
    axes_sum = (0, 1, 2)
    partial_value = jnp.stack([
        jnp.stack([jnp.sum(grad_lower * val_lower, axis=axes_sum), jnp.sum(grad_lower * val_upper, axis=axes_sum)]),
        jnp.stack([jnp.sum(grad_upper * val_upper, axis=axes_sum), jnp.sum(grad_upper * val_lower, axis=axes_sum)]),
    ])
    return prev, partial_value


def reference(acts, cotan, proj_in, proj_out, block_mix, twiddle):
    outs_mixed = []
    outs_dacts = []
    outs_win = []
    outs_wout = []
    outs_block = []
    outs_twid = []
    for section in range(SECTIONS):
        inputs = acts[section]
        grad_out = cotan[section]
        w_in = proj_in[section]
        w_out = proj_out[section]
        feature_count = inputs.shape[1]
        projected = jnp.dot(inputs, w_in, preferred_element_type=jnp.float32)
        value = projected[:, :feature_count].astype(jnp.bfloat16)
        gate = projected[:, feature_count:].astype(jnp.bfloat16)
        value_blocks = value.reshape(N_SEQ, TOK_DEV, feature_count)
        mats = block_mix[section].reshape(N_SEQ, TOK_DEV, TOK_DEV)
        blocked = jnp.einsum('pij,pjc->pic', mats.astype(jnp.float32), value_blocks.astype(jnp.float32)).astype(jnp.bfloat16)
        stored = []
        for segment_bit in range(BITS):
            stored.append(blocked)
            blocked = local_segment(blocked, twiddle[section, segment_bit], segment_bit)
        monarch = blocked.reshape(LEN, feature_count)
        hidden = (monarch.astype(jnp.float32) * gate.astype(jnp.float32)).astype(jnp.bfloat16)
        outs_mixed.append(jnp.dot(hidden, w_out, preferred_element_type=jnp.float32).astype(jnp.bfloat16))
        d_hidden = jnp.dot(grad_out, w_out.T, preferred_element_type=jnp.float32).astype(jnp.bfloat16)
        outs_wout.append(jnp.dot(hidden.T, grad_out, preferred_element_type=jnp.float32))
        d_monarch = (d_hidden.astype(jnp.float32) * gate.astype(jnp.float32)).astype(jnp.bfloat16)
        d_gate = (d_hidden.astype(jnp.float32) * monarch.astype(jnp.float32)).astype(jnp.bfloat16)
        grad_blocked = d_monarch.reshape(N_SEQ, TOK_DEV, feature_count)
        partials = [None] * BITS
        for segment_bit in range(BITS - 1, -1, -1):
            grad_blocked, partials[segment_bit] = local_back(grad_blocked, stored[segment_bit], twiddle[section, segment_bit], segment_bit)
        outs_twid.append(jnp.stack(partials))
        d_value = jnp.einsum('pij,pic->pjc', mats.astype(jnp.float32), grad_blocked.astype(jnp.float32)).astype(jnp.bfloat16)
        grad_mats = jnp.einsum('pic,pjc->pij', grad_blocked.astype(jnp.float32), value_blocks.astype(jnp.float32))
        outs_block.append(grad_mats.reshape(LEN, TOK_DEV))
        d_projected = jnp.concatenate([d_value.reshape(LEN, feature_count), d_gate], axis=1)
        outs_win.append(jnp.dot(inputs.T, d_projected, preferred_element_type=jnp.float32))
        outs_dacts.append(jnp.dot(d_projected, w_in.T, preferred_element_type=jnp.float32).astype(jnp.bfloat16))
    handed = outs_dacts[1:] + [jnp.zeros_like(outs_dacts[0])]
    return (jnp.stack(outs_mixed), jnp.stack(handed), jnp.stack(outs_win), jnp.stack(outs_wout), jnp.stack(outs_block), jnp.stack(outs_twid))
```

```python
import jax
import jax.numpy as jnp
from jax import lax
from jax.experimental import pallas as pl
from jax.experimental.pallas import tpu as pltpu
from jax.sharding import PartitionSpec as P


def from_behind(value, axis, steps):
    count = lax.axis_size(axis)
    first, last = (max(0, -steps), min(count, count - steps))
    return lax.ppermute(value, axis, [(source, source + steps) for source in range(first, last)])


def local_segment(blocked, segment_coef, segment_bit):
    block_count, inner_rows, feature_count = blocked.shape
    stride_len = 2**segment_bit
    shaped = blocked.reshape(
        block_count // (2 * stride_len), 2, stride_len, inner_rows, feature_count
    )
    lower_part = shaped[:, 0].astype(jnp.float32)
    upper_part = shaped[:, 1].astype(jnp.float32)
    new_lower = segment_coef[0, 0] * lower_part + segment_coef[0, 1] * upper_part
    new_upper = segment_coef[1, 0] * upper_part + segment_coef[1, 1] * lower_part
    joined = jnp.stack([new_lower, new_upper], axis=1)
    return joined.reshape(block_count, inner_rows, feature_count).astype(jnp.bfloat16)


def local_back(grad_blocked, stored, segment_coef, segment_bit):
    block_count, inner_rows, feature_count = grad_blocked.shape
    stride_len = 2**segment_bit
    dshape = grad_blocked.reshape(
        block_count // (2 * stride_len), 2, stride_len, inner_rows, feature_count
    )
    zshape = stored.reshape(
        block_count // (2 * stride_len), 2, stride_len, inner_rows, feature_count
    )
    grad_lower = dshape[:, 0].astype(jnp.float32)
    grad_upper = dshape[:, 1].astype(jnp.float32)
    val_lower = zshape[:, 0].astype(jnp.float32)
    val_upper = zshape[:, 1].astype(jnp.float32)
    prev_lower = segment_coef[0, 0] * grad_lower + segment_coef[1, 1] * grad_upper
    prev_upper = segment_coef[1, 0] * grad_upper + segment_coef[0, 1] * grad_lower
    joined = jnp.stack([prev_lower, prev_upper], axis=1)
    prev = joined.reshape(block_count, inner_rows, feature_count).astype(jnp.bfloat16)
    axes_sum = (0, 1, 2)
    partial_value = jnp.stack(
        [
            jnp.stack(
                [
                    jnp.sum(grad_lower * val_lower, axis=axes_sum),
                    jnp.sum(grad_lower * val_upper, axis=axes_sum),
                ]
            ),
            jnp.stack(
                [
                    jnp.sum(grad_upper * val_upper, axis=axes_sum),
                    jnp.sum(grad_upper * val_lower, axis=axes_sum),
                ]
            ),
        ]
    )
    return (prev, partial_value)


def exchange_plan(inputs, grad_out, w_in, w_out, square_mix, twiddle_w):
    row_count, feature_count = inputs.shape
    seq_count = lax.axis_size("seq")
    segment_total = seq_count.bit_length() - 1
    projected = jnp.dot(inputs, w_in, preferred_element_type=jnp.float32)
    value = projected[:, :feature_count].astype(jnp.bfloat16)
    gate = projected[:, feature_count:].astype(jnp.bfloat16)
    first_segment = jnp.dot(square_mix, value, preferred_element_type=jnp.float32).astype(
        jnp.bfloat16
    )
    partials = [None] * segment_total
    columns = lax.all_to_all(first_segment, "seq", split_axis=0, concat_axis=0, tiled=True)
    blocked = columns.reshape(seq_count, row_count // seq_count, feature_count)
    stored = []
    for segment_bit in range(segment_total):
        stored.append(blocked)
        blocked = local_segment(blocked, twiddle_w[segment_bit], segment_bit)
    monarch = lax.all_to_all(
        blocked.reshape(row_count, feature_count), "seq", split_axis=0, concat_axis=0, tiled=True
    )
    hidden = (monarch.astype(jnp.float32) * gate.astype(jnp.float32)).astype(jnp.bfloat16)
    mixed_out = jnp.dot(hidden, w_out, preferred_element_type=jnp.float32).astype(jnp.bfloat16)
    d_hidden = lax.dot_general(
        grad_out, w_out, (((1,), (1,)), ((), ())), preferred_element_type=jnp.float32
    ).astype(jnp.bfloat16)
    wout_term = lax.dot_general(
        hidden, grad_out, (((0,), (0,)), ((), ())), preferred_element_type=jnp.float32
    )
    d_monarch = (d_hidden.astype(jnp.float32) * gate.astype(jnp.float32)).astype(jnp.bfloat16)
    d_gate = (d_hidden.astype(jnp.float32) * monarch.astype(jnp.float32)).astype(jnp.bfloat16)
    grad_columns = lax.all_to_all(d_monarch, "seq", split_axis=0, concat_axis=0, tiled=True)
    grad_blocked = grad_columns.reshape(seq_count, row_count // seq_count, feature_count)
    for segment_bit in range(segment_total - 1, -1, -1):
        grad_blocked, partials[segment_bit] = local_back(
            grad_blocked, stored[segment_bit], twiddle_w[segment_bit], segment_bit
        )
    d_first = lax.all_to_all(
        grad_blocked.reshape(row_count, feature_count),
        "seq",
        split_axis=0,
        concat_axis=0,
        tiled=True,
    )
    twiddle_grad = lax.psum(jnp.stack(partials), "seq")
    d_value = lax.dot_general(
        square_mix, d_first, (((0,), (0,)), ((), ())), preferred_element_type=jnp.float32
    ).astype(jnp.bfloat16)
    grad_square = lax.dot_general(
        d_first, value, (((1,), (1,)), ((), ())), preferred_element_type=jnp.float32
    )
    d_projected = jnp.concatenate([d_value, d_gate], axis=1)
    win_term = lax.dot_general(
        inputs, d_projected, (((0,), (0,)), ((), ())), preferred_element_type=jnp.float32
    )
    win_share, wout_share = (
        lax.psum_scatter(win_term, "seq", scatter_dimension=0, tiled=True),
        lax.psum_scatter(wout_term, "seq", scatter_dimension=0, tiled=True),
    )
    input_grad = lax.dot_general(
        d_projected, w_in, (((1,), (1,)), ((), ())), preferred_element_type=jnp.float32
    ).astype(jnp.bfloat16)
    handed = from_behind(input_grad, "pipe", -1)
    return mixed_out, handed, win_share, wout_share, grad_square, twiddle_grad


def chip_hops(hops):
    return [(2 * source + core, 2 * target + core) for source, target in hops for core in (0, 1)]


CORE_SWAP = [(index, index ^ 1) for index in range(8)]
INWARD = chip_hops([(0, 1), (3, 2)])
ACROSS = chip_hops([(1, 2), (2, 1)])
OUTWARD = chip_hops([(1, 0), (2, 3)])


def hop(value, pairs):
    return lax.ppermute(value, "seq", pairs)


def dot(left, right):
    return jnp.dot(left, right, preferred_element_type=jnp.float32)


def dot_rows(left, right):
    return lax.dot_general(
        left, right, (((0,), (0,)), ((), ())), preferred_element_type=jnp.float32
    )


def dot_columns(left, right):
    return lax.dot_general(
        left, right, (((1,), (1,)), ((), ())), preferred_element_type=jnp.float32
    )


def narrow(value):
    return value.astype(jnp.bfloat16)


def wide(value):
    return value.astype(jnp.float32)


def coef_at(coef_ref, bit, side, term):
    return coef_ref[pl.ds(4 * bit + 2 * side + term, 1), :]


def forward_kernel(coef_ref, *refs):
    seg0 = refs[0:4]
    swapped = refs[4:8]
    gates = refs[8:12]
    seg1_out, seg2_out, seg3_out, hidden_out = refs[12:16]
    first = []
    for k in range(4):
        own, other = wide(seg0[k][...]), wide(swapped[k][...])
        first.append(narrow(coef_at(coef_ref, 0, 0, 0) * own + coef_at(coef_ref, 0, 0, 1) * other))
    for k in range(2):
        seg1_out[k] = first[k]
    first = [wide(part) for part in first]
    second = []
    for k in range(4):
        side = k & 1
        second.append(
            narrow(
                coef_at(coef_ref, 1, side, 0) * first[k]
                + coef_at(coef_ref, 1, side, 1) * first[k ^ 1]
            )
        )
        seg2_out[k] = second[k]
    second = [wide(part) for part in second]
    for k in range(4):
        side = k >> 1
        third = narrow(
            coef_at(coef_ref, 2, side, 0) * second[k]
            + coef_at(coef_ref, 2, side, 1) * second[k ^ 2]
        )
        seg3_out[k] = third
        hidden_out[k] = narrow(wide(third) * wide(gates[k][...]))


def row_groups(value):
    rows, columns = value.shape
    return value.reshape(rows // 8, 8, columns).sum(axis=0)


def backward_kernel(coef_ref, *refs):
    d_hidden = refs[0:4]
    gates = refs[4:8]
    seg1_ref, seg2_ref, seg3_ref = refs[8:11]
    d_gate_out, d_seg1_out, partial_out = refs[11:14]

    @pl.when(pl.program_id(0) == 0)
    def _():
        partial_out[...] = jnp.zeros_like(partial_out)

    third = []
    for k in range(4):
        grad = wide(d_hidden[k][...])
        d_gate_out[k] = narrow(grad * wide(seg3_ref[k]))
        third.append(wide(narrow(grad * wide(gates[k][...]))))
    for k in range(2):
        partial_out[4] += row_groups(third[k] * wide(seg2_ref[k]))
        partial_out[5] += row_groups(third[k] * wide(seg2_ref[k ^ 2]))
    second = []
    for k in range(4):
        side = k >> 1
        second.append(
            wide(
                narrow(
                    coef_at(coef_ref, 2, side, 0) * third[k]
                    + coef_at(coef_ref, 2, 1 - side, 1) * third[k ^ 2]
                )
            )
        )
    for k in range(2):
        partial_out[2 * k] += row_groups(second[k] * wide(seg1_ref[k]))
        partial_out[2 * k + 1] += row_groups(second[k] * wide(seg1_ref[k ^ 1]))
    for k in range(4):
        side = k & 1
        d_seg1_out[k] = narrow(
            coef_at(coef_ref, 1, side, 0) * second[k]
            + coef_at(coef_ref, 1, 1 - side, 1) * second[k ^ 1]
        )


def first_bit_kernel(coef_ref, *refs):
    d_seg1_ref, d_swapped_ref = refs[0:2]
    seg0 = refs[2:4]
    swapped = refs[4:6]
    d_seg0_out, partial_out = refs[6:8]

    @pl.when(pl.program_id(0) == 0)
    def _():
        partial_out[...] = jnp.zeros_like(partial_out)

    for k in range(4):
        own, other = wide(d_seg1_ref[k]), wide(d_swapped_ref[k])
        d_seg0_out[k] = narrow(
            coef_at(coef_ref, 0, 0, 0) * own + coef_at(coef_ref, 0, 1, 1) * other
        )
        if k < 2:
            partial_out[0] += row_groups(own * wide(seg0[k][...]))
            partial_out[1] += row_groups(own * wide(swapped[k][...]))


TILE = 32


def tile(columns, column_at=0, row_at=0):
    return pl.BlockSpec((TILE, columns), lambda i: (i + row_at, column_at))


def stacked(count, columns, row_at=0):
    return pl.BlockSpec((count, TILE, columns), lambda i: (0, i + row_at, 0))


def whole(*shape):
    return pl.BlockSpec(shape, lambda i: (0,) * len(shape))


def shape_of(kind, *shape):
    return jax.ShapeDtypeStruct(shape, kind)


def relay_plan(inputs, grad_out, w_in, w_out, mix, twiddle_w):
    rows, width = inputs.shape
    share = width // 8
    place = lax.axis_index("seq")
    chip, core = place // 2, place % 2
    inner = (chip == 1) | (chip == 2)
    flips = (core, chip & 1, chip >> 1)
    coefs = jnp.concatenate(
        [
            jnp.where(flips[bit] == 1, twiddle_w[bit][::-1], twiddle_w[bit]).reshape(4, width)
            for bit in range(3)
        ]
        + [jnp.zeros((4, width), jnp.float32)]
    )
    half = rows // 2

    def everywhere(value):
        outer = hop(value, INWARD)
        return [value, outer, hop(outer, ACROSS), hop(value, ACROSS)]

    mixes = everywhere(mix)
    acts = everywhere(inputs)
    cotans = [everywhere(grad_out[h * half : (h + 1) * half]) for h in range(2)]

    projected = [narrow(dot(part, w_in)) for part in acts]
    values = [part[:, :width] for part in projected]
    seg0 = [narrow(dot(mixes[k], values[k])) for k in range(4)]
    swapped = [hop(part, CORE_SWAP) for part in seg0]

    bf16, f32 = jnp.bfloat16, jnp.float32
    seg1, seg2, seg3, hidden = pl.pallas_call(
        forward_kernel,
        grid=(rows // TILE,),
        in_specs=[whole(16, width)] + [tile(width)] * 8 + [tile(width, 1)] * 4,
        out_specs=[stacked(2, width)] + [stacked(4, width)] * 3,
        out_shape=[shape_of(bf16, 2, rows, width)] + [shape_of(bf16, 4, rows, width)] * 3,
        cost_estimate=pl.CostEstimate(
            flops=16 * rows * width, bytes_accessed=52 * rows * width, transcendentals=0
        ),
        compiler_params=pltpu.CompilerParams(vmem_limit_bytes=40 * 2**20),
        name="forward_segments",
    )(coefs, *seg0, *swapped, *projected)

    def row_shares(value, axis):
        pieces = []
        for core_bit in (0, 1):
            for chip_bit in (0, 1):
                owner = 2 * (chip ^ chip_bit) + (core ^ core_bit)
                pieces.append(lax.dynamic_slice_in_dim(value, owner * share, share, axis))
        return jnp.concatenate(pieces, axis=axis)

    act_columns = [row_shares(part, 1) for part in acts]
    mixed_columns = [narrow(dot(mixes[k], act_columns[k])) for k in range(4)]
    hidden_columns = row_shares(hidden, 2)

    def half_of(parts, h):
        return jnp.concatenate([part[h * half : (h + 1) * half] for part in parts], axis=0)

    win_value, win_gate, wout, twiddle_parts, first_grads = 0.0, 0.0, 0.0, 0.0, []
    for h in range(2):
        at = h * (half // TILE)
        d_hidden = [narrow(dot_columns(part, w_out)) for part in cotans[h]]
        d_gate, d_seg1, later_part = pl.pallas_call(
            backward_kernel,
            grid=(half // TILE,),
            in_specs=[whole(16, width)]
            + [tile(width)] * 4
            + [tile(width, 1, at)] * 4
            + [stacked(2, width, at), stacked(4, width, at), stacked(4, width, at)],
            out_specs=[stacked(4, width), stacked(4, width), whole(6, 8, width)],
            out_shape=[
                shape_of(bf16, 4, half, width),
                shape_of(bf16, 4, half, width),
                shape_of(f32, 6, 8, width),
            ],
            cost_estimate=pl.CostEstimate(
                flops=20 * half * width, bytes_accessed=52 * half * width, transcendentals=0
            ),
            compiler_params=pltpu.CompilerParams(vmem_limit_bytes=40 * 2**20),
            name="backward_segments",
        )(coefs, *d_hidden, *projected, seg1, seg2, seg3)
        d_swapped = hop(d_seg1, CORE_SWAP)
        d_seg0, first_part = pl.pallas_call(
            first_bit_kernel,
            grid=(half // TILE,),
            in_specs=[whole(16, width)]
            + [stacked(4, width)] * 2
            + [tile(width, 0, at)] * 4,
            out_specs=[stacked(4, width), whole(2, 8, width)],
            out_shape=[shape_of(bf16, 4, half, width), shape_of(f32, 2, 8, width)],
            cost_estimate=pl.CostEstimate(
                flops=20 * half * width, bytes_accessed=32 * half * width, transcendentals=0
            ),
            compiler_params=pltpu.CompilerParams(vmem_limit_bytes=40 * 2**20),
            name="first_segment_grad",
        )(coefs, d_seg1, d_swapped, *seg0[:2], *swapped[:2])
        first_grads.append(d_seg0)
        d_gate_rows = d_gate.reshape(4 * half, width)
        d_seg0_rows = d_seg0.reshape(4 * half, width)
        hidden_rows = hidden_columns[:, h * half : (h + 1) * half].reshape(4 * half, width // 2)
        win_gate += dot_rows(half_of(act_columns, h), d_gate_rows)
        win_value += dot_rows(half_of(mixed_columns, h), d_seg0_rows)
        wout += dot_rows(hidden_rows, jnp.concatenate(cotans[h], axis=0))
        twiddle_parts += jnp.concatenate([first_part, later_part], axis=0).sum(axis=1)

    def combine(term):
        kept = 2 * share
        total = term[:kept] + wide(hop(narrow(term[kept:]), CORE_SWAP))
        arrived = wide(hop(narrow(total[share:]), OUTWARD))
        return jnp.where(inner, total[:share], arrived)

    wout_share = combine(wout)
    gate_share = combine(win_gate)
    value_share = combine(win_value)

    def one_side(pair, flip):
        empty = jnp.zeros_like(pair)
        return jnp.where(flip == 1, jnp.stack([empty, pair]), jnp.stack([pair, empty]))

    both = twiddle_parts[2:6].reshape(2, 2, width)
    terms = jnp.stack(
        [
            one_side(twiddle_parts[0:2], flips[0]),
            jnp.where(flips[1] == 1, both[::-1], both),
            one_side(twiddle_parts[6:8], flips[2]),
        ]
    )
    terms = terms + hop(terms, CORE_SWAP)
    terms = terms + hop(terms, ACROSS)
    twiddle_grad = jnp.where(inner, terms, hop(terms, OUTWARD))

    monarch = jnp.where(inner, seg3[0], hop(seg3[1], OUTWARD))
    gate = projected[0][:, width:]
    mixed_out = narrow(dot(narrow(wide(monarch) * wide(gate)), w_out))
    own_d_hidden = narrow(dot_columns(grad_out, w_out))
    own_d_gate = narrow(wide(own_d_hidden) * wide(monarch))
    own_d_first = jnp.concatenate(
        [jnp.where(inner, part[0], hop(part[1], OUTWARD)) for part in first_grads], axis=0
    )
    d_value = narrow(dot_rows(mix, own_d_first))
    grad_square = dot_columns(own_d_first, values[0])
    input_grad = narrow(
        dot_columns(d_value, w_in[:, :width]) + dot_columns(own_d_gate, w_in[:, width:])
    )
    handed = from_behind(input_grad, "pipe", -1)
    win_share = jnp.concatenate([value_share, gate_share], axis=1)
    return mixed_out, handed, win_share, wout_share, grad_square, twiddle_grad


def on_device(*arguments):
    plan = relay_plan if lax.axis_size("seq") == 8 else exchange_plan
    return tuple(result[None] for result in plan(*(part[0] for part in arguments)))


def solution(mesh):
    in_specs = (
        P("pipe", "seq", None),
        P("pipe", "seq", None),
        P("pipe", None, None),
        P("pipe", None, None),
        P("pipe", "seq", None),
        P("pipe", None, None, None, None),
    )
    out_specs = (
        P("pipe", "seq", None),
        P("pipe", "seq", None),
        P("pipe", "seq", None),
        P("pipe", "seq", None),
        P("pipe", "seq", None),
        P("pipe", None, None, None, None),
    )
    return jax.shard_map(
        on_device, mesh=mesh, in_specs=in_specs, out_specs=out_specs, check_vma=False
    )
```

```python
import functools

import jax
import jax.numpy as jnp
from jax import lax
from jax.experimental import pallas as pl
from jax.experimental.pallas import tpu as pltpu
from jax.sharding import PartitionSpec as P


def from_behind(value, axis, steps):
    count = lax.axis_size(axis)
    first, last = (max(0, -steps), min(count, count - steps))
    return lax.ppermute(value, axis, [(source, source + steps) for source in range(first, last)])


def local_segment(blocked, segment_coef, segment_bit):
    block_count, inner_rows, feature_count = blocked.shape
    stride_len = 2**segment_bit
    shaped = blocked.reshape(
        block_count // (2 * stride_len), 2, stride_len, inner_rows, feature_count
    )
    lower_part = shaped[:, 0].astype(jnp.float32)
    upper_part = shaped[:, 1].astype(jnp.float32)
    new_lower = segment_coef[0, 0] * lower_part + segment_coef[0, 1] * upper_part
    new_upper = segment_coef[1, 0] * upper_part + segment_coef[1, 1] * lower_part
    joined = jnp.stack([new_lower, new_upper], axis=1)
    return joined.reshape(block_count, inner_rows, feature_count).astype(jnp.bfloat16)


def local_back(grad_blocked, stored, segment_coef, segment_bit):
    block_count, inner_rows, feature_count = grad_blocked.shape
    stride_len = 2**segment_bit
    dshape = grad_blocked.reshape(
        block_count // (2 * stride_len), 2, stride_len, inner_rows, feature_count
    )
    zshape = stored.reshape(
        block_count // (2 * stride_len), 2, stride_len, inner_rows, feature_count
    )
    grad_lower = dshape[:, 0].astype(jnp.float32)
    grad_upper = dshape[:, 1].astype(jnp.float32)
    val_lower = zshape[:, 0].astype(jnp.float32)
    val_upper = zshape[:, 1].astype(jnp.float32)
    prev_lower = segment_coef[0, 0] * grad_lower + segment_coef[1, 1] * grad_upper
    prev_upper = segment_coef[1, 0] * grad_upper + segment_coef[0, 1] * grad_lower
    joined = jnp.stack([prev_lower, prev_upper], axis=1)
    prev = joined.reshape(block_count, inner_rows, feature_count).astype(jnp.bfloat16)
    axes_sum = (0, 1, 2)
    partial_value = jnp.stack(
        [
            jnp.stack(
                [
                    jnp.sum(grad_lower * val_lower, axis=axes_sum),
                    jnp.sum(grad_lower * val_upper, axis=axes_sum),
                ]
            ),
            jnp.stack(
                [
                    jnp.sum(grad_upper * val_upper, axis=axes_sum),
                    jnp.sum(grad_upper * val_lower, axis=axes_sum),
                ]
            ),
        ]
    )
    return (prev, partial_value)


def exchange_plan(inputs, grad_out, w_in, w_out, square_mix, twiddle_w):
    row_count, feature_count = inputs.shape
    seq_count = lax.axis_size("seq")
    segment_total = seq_count.bit_length() - 1
    projected = jnp.dot(inputs, w_in, preferred_element_type=jnp.float32)
    value = projected[:, :feature_count].astype(jnp.bfloat16)
    gate = projected[:, feature_count:].astype(jnp.bfloat16)
    first_segment = jnp.dot(square_mix, value, preferred_element_type=jnp.float32).astype(
        jnp.bfloat16
    )
    partials = [None] * segment_total
    columns = lax.all_to_all(first_segment, "seq", split_axis=0, concat_axis=0, tiled=True)
    blocked = columns.reshape(seq_count, row_count // seq_count, feature_count)
    stored = []
    for segment_bit in range(segment_total):
        stored.append(blocked)
        blocked = local_segment(blocked, twiddle_w[segment_bit], segment_bit)
    monarch = lax.all_to_all(
        blocked.reshape(row_count, feature_count), "seq", split_axis=0, concat_axis=0, tiled=True
    )
    hidden = (monarch.astype(jnp.float32) * gate.astype(jnp.float32)).astype(jnp.bfloat16)
    mixed_out = jnp.dot(hidden, w_out, preferred_element_type=jnp.float32).astype(jnp.bfloat16)
    d_hidden = lax.dot_general(
        grad_out, w_out, (((1,), (1,)), ((), ())), preferred_element_type=jnp.float32
    ).astype(jnp.bfloat16)
    wout_term = lax.dot_general(
        hidden, grad_out, (((0,), (0,)), ((), ())), preferred_element_type=jnp.float32
    )
    d_monarch = (d_hidden.astype(jnp.float32) * gate.astype(jnp.float32)).astype(jnp.bfloat16)
    d_gate = (d_hidden.astype(jnp.float32) * monarch.astype(jnp.float32)).astype(jnp.bfloat16)
    grad_columns = lax.all_to_all(d_monarch, "seq", split_axis=0, concat_axis=0, tiled=True)
    grad_blocked = grad_columns.reshape(seq_count, row_count // seq_count, feature_count)
    for segment_bit in range(segment_total - 1, -1, -1):
        grad_blocked, partials[segment_bit] = local_back(
            grad_blocked, stored[segment_bit], twiddle_w[segment_bit], segment_bit
        )
    d_first = lax.all_to_all(
        grad_blocked.reshape(row_count, feature_count),
        "seq",
        split_axis=0,
        concat_axis=0,
        tiled=True,
    )
    twiddle_grad = lax.psum(jnp.stack(partials), "seq")
    d_value = lax.dot_general(
        square_mix, d_first, (((0,), (0,)), ((), ())), preferred_element_type=jnp.float32
    ).astype(jnp.bfloat16)
    grad_square = lax.dot_general(
        d_first, value, (((1,), (1,)), ((), ())), preferred_element_type=jnp.float32
    )
    d_projected = jnp.concatenate([d_value, d_gate], axis=1)
    win_term = lax.dot_general(
        inputs, d_projected, (((0,), (0,)), ((), ())), preferred_element_type=jnp.float32
    )
    win_share, wout_share = (
        lax.psum_scatter(win_term, "seq", scatter_dimension=0, tiled=True),
        lax.psum_scatter(wout_term, "seq", scatter_dimension=0, tiled=True),
    )
    input_grad = lax.dot_general(
        d_projected, w_in, (((1,), (1,)), ((), ())), preferred_element_type=jnp.float32
    ).astype(jnp.bfloat16)
    handed = from_behind(input_grad, "pipe", -1)
    return mixed_out, handed, win_share, wout_share, grad_square, twiddle_grad


def chip_hops(hops):
    return [(2 * source + core, 2 * target + core) for source, target in hops for core in (0, 1)]


CORE_SWAP = [(index, index ^ 1) for index in range(8)]
INWARD = chip_hops([(0, 1), (3, 2)])
ACROSS = chip_hops([(1, 2), (2, 1)])
OUTWARD = chip_hops([(1, 0), (2, 3)])


def relay_back(outward):
    return [
        (8 * (section + 1) + source, 8 * section + target)
        for section in range(lax.axis_size("pipe") - 1)
        for source, target in (OUTWARD if outward else [(place, place) for place in range(2, 6)])
    ]


def hop(value, pairs):
    return lax.ppermute(value, "seq", pairs)


def dot(left, right):
    return jnp.dot(left, right, preferred_element_type=jnp.float32)


def dot_rows(left, right):
    return lax.dot_general(
        left, right, (((0,), (0,)), ((), ())), preferred_element_type=jnp.float32
    )


def dot_columns(left, right):
    return lax.dot_general(
        left, right, (((1,), (1,)), ((), ())), preferred_element_type=jnp.float32
    )


def narrow(value):
    return value.astype(jnp.bfloat16)


def wide(value):
    return value.astype(jnp.float32)


def coef_at(coef_ref, bit, side, term):
    return coef_ref[pl.ds(4 * bit + 2 * side + term, 1), :]


def cross(coef_ref, bit, side, own, other):
    return coef_at(coef_ref, bit, side, 0) * own + coef_at(coef_ref, bit, side, 1) * other


def cross_back(coef_ref, bit, side, own, other):
    return coef_at(coef_ref, bit, side, 0) * own + coef_at(coef_ref, bit, 1 - side, 1) * other


def pack_kernel(acts_ref, mix_ref, pack_ref):
    rows, width = acts_ref.shape
    depth = mix_ref.shape[1]
    piece = rows * depth // width
    pack_ref[pl.ds(0, rows), :] = acts_ref[...]
    for i in range(rows // piece):
        pack_ref[pl.ds(rows, piece), pl.ds(i * depth, depth)] = mix_ref[pl.ds(i * piece, piece), :]


def unpack_mix(pack_ref, rows):
    piece = pack_ref.shape[0] - rows
    return jnp.concatenate(
        [pack_ref[pl.ds(rows, piece), pl.ds(i * rows, rows)] for i in range(rows // piece)], axis=0
    )


def block_kernel(starts_ref, pack_ref, weight_ref, columns_ref, mixed_ref, seg0_ref, gate_ref, *value):
    rows, width = gate_ref.shape
    half, share = width // 2, width // 8
    acts = pack_ref[pl.ds(0, rows), :]
    mix = unpack_mix(pack_ref, rows)
    for i in range(4):
        product = narrow(dot(acts, weight_ref[:, pl.ds(i * half, half)]))
        if i < 2:
            seg0_ref[:, pl.ds(i * half, half)] = narrow(dot(mix, product))
            if value:
                value[0][:, pl.ds(i * half, half)] = product
        else:
            gate_ref[:, pl.ds((i - 2) * half, half)] = product
    for j in range(4):
        start = pl.multiple_of(starts_ref[j], share)
        columns_ref[:, pl.ds(j * share, share)] = pack_ref[pl.ds(0, rows), pl.ds(start, share)]
    mixed_ref[...] = narrow(dot(mix, columns_ref[...]))


def d_hidden_kernel(weight_ref, *refs):
    for cotan_ref, out_ref in zip(refs[: len(refs) // 2], refs[len(refs) // 2 :]):
        out_ref[...] = narrow(dot_columns(cotan_ref[...], weight_ref[...]))


def early_grads_kernel(*refs):
    columns, d_gate_ref, hidden_ref, cotans = refs[0:4], refs[4], refs[5], refs[6:10]
    given_ref, kept_ref = refs[10:12]
    half = columns[0].shape[1] // 2
    for part in range(2):
        gate_total, out_total = 0.0, 0.0
        cut = pl.ds(part * half, half)
        for k in range(4):
            gate_total += dot_rows(columns[k][:, cut], d_gate_ref[k])
            out_total += dot_rows(hidden_ref[k, :, cut], cotans[k][...])
        if part == 0:
            given_ref[pl.ds(0, half), :] = narrow(gate_total)
            given_ref[pl.ds(half, half), :] = narrow(out_total)
        else:
            kept_ref[pl.ds(0, half), :] = gate_total
            kept_ref[pl.ds(half, half), :] = out_total


def late_grads_kernel(*refs):
    mixed, d_seg0_ref, given_ref, kept_ref = refs[0:4], refs[4], refs[5], refs[6]
    half = given_ref.shape[0]
    for part in range(2):
        total = 0.0
        for k in range(4):
            total += dot_rows(mixed[k][:, pl.ds(part * half, half)], d_seg0_ref[k])
        if part == 0:
            given_ref[...] = narrow(total)
        else:
            kept_ref[...] = total


def sums_kernel(kept_ref, got_ref, out_ref):
    share = out_ref.shape[0] // (kept_ref.shape[0] // 256)
    for i in range(kept_ref.shape[0] // (2 * share)):
        there = pl.ds((2 * i + 1) * share, share)
        out_ref[pl.ds(i * share, share), :] = narrow(kept_ref[there, :] + wide(got_ref[there, :]))


def own_kernel(d_seg0_ref, d_gate_ref, weight_ref, *refs):
    packs, values, d_acts, squares = refs[0:2], refs[2:4], refs[4:6], refs[6:8]
    rows, width = values[0].shape
    for k in range(2):
        d_seg0 = d_seg0_ref[k]
        d_value = narrow(dot_rows(unpack_mix(packs[k], rows), d_seg0))
        d_acts[k][...] = narrow(
            dot_columns(d_value, weight_ref[:, pl.ds(0, width)])
            + dot_columns(d_gate_ref[k], weight_ref[:, pl.ds(width, width)])
        )
        squares[k][...] = dot_columns(d_seg0, values[k][...])


def mixed_kernel(hidden_ref, weight_ref, *outs):
    for k in range(2):
        outs[k][...] = narrow(dot(hidden_ref[k], weight_ref[...]))


def forward_kernel(starts_ref, coef_ref, *refs):
    seg0 = refs[0:4]
    swapped = refs[4:8]
    gates = refs[8:12]
    seg1_out, seg2_out, hidden_out, columns_out, held = refs[12:17]
    share = coef_ref.shape[1] // 8
    first = [cross(coef_ref, 0, 0, seg0[k][...], swapped[k][...]) for k in range(4)]
    for k in range(2):
        seg1_out[k] = first[k]
    second = [cross(coef_ref, 1, k & 1, first[k], first[k ^ 1]) for k in range(4)]
    for k in range(4):
        seg2_out[k] = second[k]
    for k in range(4):
        hidden = cross(coef_ref, 2, k >> 1, second[k], second[k ^ 2]) * gates[k][...]
        held[k] = hidden
        if k < 2:
            hidden_out[k] = hidden
    for k in range(4):
        for j in range(4):
            start = pl.multiple_of(starts_ref[j], share)
            columns_out[k, :, pl.ds(j * share, share)] = held[k, :, pl.ds(start, share)]


def row_sums(value):
    return dot(jnp.ones((8, value.shape[0]), value.dtype), value)


def backward_kernel(coef_ref, *refs):
    d_hidden = refs[0:4]
    gates = refs[4:8]
    seg1_ref, seg2_ref = refs[8:10]
    d_gate_out, d_seg1_out, partial_out = refs[10:13]

    @pl.when(pl.program_id(0) == 0)
    def _():
        partial_out[...] = jnp.zeros_like(partial_out)

    third = []
    for k in range(4):
        grad = d_hidden[k][...]
        d_gate_out[k] = grad * cross(coef_ref, 2, k >> 1, seg2_ref[k], seg2_ref[k ^ 2])
        third.append(grad * gates[k][...])
    for k in range(2):
        partial_out[4] += row_sums(third[k] * seg2_ref[k])
        partial_out[5] += row_sums(third[k] * seg2_ref[k ^ 2])
    second = [cross_back(coef_ref, 2, k >> 1, third[k], third[k ^ 2]) for k in range(4)]
    for k in range(2):
        partial_out[2 * k] += row_sums(second[k] * seg1_ref[k])
        partial_out[2 * k + 1] += row_sums(second[k] * seg1_ref[k ^ 1])
    for k in range(4):
        d_seg1_out[k] = cross_back(coef_ref, 1, k & 1, second[k], second[k ^ 1])


def first_bit_kernel(coef_ref, *refs):
    d_seg1_ref, d_swapped_ref = refs[0:2]
    seg0 = refs[2:4]
    swapped = refs[4:6]
    d_seg0_out, partial_out = refs[6:8]

    @pl.when(pl.program_id(0) == 0)
    def _():
        partial_out[...] = jnp.zeros_like(partial_out)

    for k in range(4):
        own, other = d_seg1_ref[k], d_swapped_ref[k]
        d_seg0 = cross_back(coef_ref, 0, 0, own, other)
        d_seg0_out[k] = d_seg0
        if k < 2:
            partial_out[0] += row_sums(own * seg0[k][...])
            partial_out[1] += row_sums(own * swapped[k][...])


TILE = 64


def tile(columns, column_at=0, row_at=0):
    return pl.BlockSpec((TILE, columns), lambda i: (i + row_at, column_at))


def stacked(count, columns, row_at=0):
    return pl.BlockSpec((count, TILE, columns), lambda i: (0, i + row_at, 0))


def whole(*shape):
    return pl.BlockSpec(shape, lambda i: (0,) * len(shape))


def shape_of(kind, *shape):
    return jax.ShapeDtypeStruct(shape, kind)


def kernel_call(kernel, name, work=1, **settings):
    return pl.pallas_call(
        kernel,
        cost_estimate=pl.CostEstimate(flops=work, bytes_accessed=1, transcendentals=0),
        compiler_params=pltpu.CompilerParams(vmem_limit_bytes=16 * 2**20),
        name=name,
        **settings,
    )


def in_place(kernel, name, operands, *outs, work=1, scalars=0):
    local = pl.BlockSpec(memory_space=pltpu.VMEM)
    return kernel_call(
        kernel,
        name,
        work,
        in_specs=[pl.BlockSpec(memory_space=pltpu.SMEM)] * scalars
        + [local] * (len(operands) - scalars),
        out_specs=[local] * len(outs),
        out_shape=list(outs),
    )(*operands)


def after(value, *earlier):
    return lax.optimization_barrier((value, *earlier))[0]


def relay_plan(inputs, grad_out, w_in, w_out, mix, twiddle_w):
    rows, width = inputs.shape
    share = width // 8
    bf16, f32 = jnp.bfloat16, jnp.float32
    place = lax.axis_index("seq")
    chip, core = place // 2, place % 2
    inner = (chip == 1) | (chip == 2)
    flips = (core, chip & 1, chip >> 1)
    scalar = pl.BlockSpec(memory_space=pltpu.SMEM)

    starts = jnp.stack(
        [
            (2 * (chip ^ chip_bit) + (core ^ core_bit)) * share
            for core_bit in (1, 0)
            for chip_bit in (0, 1)
        ]
    ).astype(jnp.int32)

    full, narrow_full = shape_of(bf16, rows, width), shape_of(bf16, rows, width // 2)
    packed_rows = rows + mix.size // width
    pack = kernel_call(pack_kernel, "pack", out_shape=shape_of(bf16, packed_rows, width))(
        inputs, mix
    )

    def block(k, packed, work=1):
        return in_place(
            block_kernel,
            f"block_{k}",
            [starts, packed, w_in],
            *([narrow_full] * 2 + [full] * (2 + (k < 2))),
            work=work,
            scalars=1,
        )

    outer_pack, across_pack = hop(pack, INWARD), hop(pack, ACROSS)
    own = block(0, pack, 4 * rows * width * width)
    (d_hidden_own,) = in_place(
        d_hidden_kernel, "d_hidden", [w_out, grad_out], full, work=2 * rows * width * width
    )
    far_pack = hop(after(outer_pack, own[0], d_hidden_own), ACROSS)
    outer_cotan = hop(after(grad_out, outer_pack), INWARD)
    across_cotan = hop(after(grad_out, outer_pack), ACROSS)
    far_cotan = hop(outer_cotan, ACROSS)
    outer = block(1, outer_pack)
    across = block(3, after(across_pack, outer[0]))
    far = block(2, after(far_pack, outer_cotan, across[0]))

    coefs = jnp.concatenate(
        [
            jnp.where(flips[bit] == 1, twiddle_w[bit][::-1], twiddle_w[bit]).reshape(4, width)
            for bit in range(3)
        ]
        + [jnp.zeros((4, width), jnp.float32)]
    ).astype(bf16)
    blocks = [own, outer, far, across]
    seg0 = [part[2] for part in blocks]
    gates = [part[3] for part in blocks]
    swapped = [hop(part, CORE_SWAP) for part in seg0]
    seg1, seg2, hidden, hidden_columns = kernel_call(
        forward_kernel,
        "forward_segments",
        grid=(rows // TILE,),
        in_specs=[scalar, whole(16, width)] + [tile(width)] * 12,
        out_specs=[
            stacked(2, width),
            stacked(4, width),
            stacked(2, width),
            stacked(4, width // 2),
        ],
        out_shape=[
            shape_of(bf16, 2, rows, width),
            shape_of(bf16, 4, rows, width),
            shape_of(bf16, 2, rows, width),
            shape_of(bf16, 4, rows, width // 2),
        ],
        scratch_shapes=[pltpu.VMEM((4, TILE, width), bf16)],
    )(starts, coefs, *seg0, *swapped, *gates)
    d_hidden_outer, d_hidden_across = in_place(
        d_hidden_kernel,
        "d_hidden",
        [w_out, outer_cotan, after(across_cotan, hidden)],
        full,
        full,
    )
    own_mixed, outer_mixed = in_place(mixed_kernel, "mixed", [hidden, w_out], full, full)
    sent_mixed = hop(outer_mixed, OUTWARD)

    far_cotan = after(far_cotan, outer_mixed, d_hidden_outer)
    (d_hidden_far,) = in_place(d_hidden_kernel, "d_hidden", [w_out, far_cotan], full)
    d_hidden = [d_hidden_own, d_hidden_outer, d_hidden_far, d_hidden_across]
    d_gate, d_seg1, later_part = kernel_call(
        backward_kernel,
        "backward_segments",
        grid=(rows // TILE,),
        in_specs=[whole(16, width)]
        + [tile(width)] * 8
        + [stacked(2, width), stacked(4, width)],
        out_specs=[stacked(4, width), stacked(4, width), whole(6, 8, width)],
        out_shape=[shape_of(bf16, 4, rows, width)] * 2 + [shape_of(f32, 6, 8, width)],
    )(coefs, *d_hidden, *gates, seg1, seg2)
    d_swapped = hop(d_seg1, CORE_SWAP)

    early_given, early_kept = in_place(
        early_grads_kernel,
        "early_grads",
        [part[0] for part in blocks]
        + [d_gate, hidden_columns, grad_out, outer_cotan, far_cotan, across_cotan],
        shape_of(bf16, 4 * share, width),
        shape_of(f32, 4 * share, width),
    )
    early_got = hop(early_given, CORE_SWAP)
    (early_sums,) = in_place(
        sums_kernel, "early_sums", [early_kept, early_got], shape_of(bf16, 2 * share, width)
    )
    sent_early = hop(early_sums, OUTWARD)
    d_seg0, first_part = kernel_call(
        first_bit_kernel,
        "first_segment_grad",
        grid=(rows // TILE,),
        in_specs=[whole(16, width)] + [stacked(4, width)] * 2 + [tile(width)] * 4,
        out_specs=[stacked(4, width), whole(2, 8, width)],
        out_shape=[shape_of(bf16, 4, rows, width), shape_of(f32, 2, 8, width)],
    )(coefs, d_seg1, after(d_swapped, early_sums), *seg0[:2], *swapped[:2])
    late_given, late_kept = in_place(
        late_grads_kernel,
        "late_grads",
        [part[1] for part in blocks] + [d_seg0],
        shape_of(bf16, 2 * share, width),
        shape_of(f32, 2 * share, width),
    )
    late_got = hop(late_given, CORE_SWAP)
    own_d_acts, outer_d_acts, own_square, outer_square = in_place(
        own_kernel,
        "own_grads",
        [after(d_seg0, late_given), d_gate, w_in, pack, outer_pack, own[4], outer[4]],
        full,
        full,
        shape_of(f32, rows, rows),
        shape_of(f32, rows, rows),
    )
    (late_sums,) = in_place(
        sums_kernel, "late_sums", [late_kept, late_got], shape_of(bf16, share, width)
    )
    sent_late = hop(late_sums, OUTWARD)
    sent_square = hop(narrow(outer_square), OUTWARD)
    own_handed = lax.ppermute(own_d_acts, ("pipe", "seq"), relay_back(False))
    outer_handed = lax.ppermute(outer_d_acts, ("pipe", "seq"), relay_back(True))

    def one_side(pair_terms, flip):
        empty = jnp.zeros_like(pair_terms)
        return jnp.where(
            flip == 1, jnp.stack([empty, pair_terms]), jnp.stack([pair_terms, empty])
        )

    first_terms, later_terms = after(first_part[:, 0], late_sums), after(later_part[:, 0], late_sums)
    both = later_terms[:4].reshape(2, 2, width)
    terms = jnp.stack(
        [
            one_side(first_terms, flips[0]),
            jnp.where(flips[1] == 1, both[::-1], both),
            one_side(later_terms[4:], flips[2]),
        ]
    )
    terms = terms + hop(terms, CORE_SWAP)
    terms = terms + hop(terms, ACROSS)
    twiddle_grad = jnp.where(inner, terms, hop(terms, OUTWARD))

    mixed_out = jnp.where(inner, own_mixed, after(sent_mixed, late_sums))
    handed = jnp.where(inner, own_handed, outer_handed)
    grad_square = jnp.where(inner, own_square, wide(sent_square))
    sent_early = wide(after(sent_early, twiddle_grad))
    sent_late = wide(after(sent_late, twiddle_grad))

    def share_of(kept, got, sent, at):
        here = slice(2 * at * share, (2 * at + 1) * share)
        mine = kept[here] + wide(got[here])
        return jnp.where(inner, mine, sent[at * share : (at + 1) * share])

    win_share = jnp.concatenate(
        [share_of(late_kept, late_got, sent_late, 0), share_of(early_kept, early_got, sent_early, 0)],
        axis=1,
    )
    wout_share = share_of(early_kept, early_got, sent_early, 1)
    return mixed_out, handed, win_share, wout_share, grad_square, twiddle_grad


def on_device(*arguments):
    plan = relay_plan if lax.axis_size("seq") == 8 else exchange_plan
    return tuple(result[None] for result in plan(*(part[0] for part in arguments)))


def solution(mesh):
    in_specs = (
        P("pipe", "seq", None),
        P("pipe", "seq", None),
        P("pipe", None, None),
        P("pipe", None, None),
        P("pipe", "seq", None),
        P("pipe", None, None, None, None),
    )
    out_specs = (
        P("pipe", "seq", None),
        P("pipe", "seq", None),
        P("pipe", "seq", None),
        P("pipe", "seq", None),
        P("pipe", "seq", None),
        P("pipe", None, None, None, None),
    )
    return jax.shard_map(
        on_device, mesh=mesh, in_specs=in_specs, out_specs=out_specs, check_vma=False
    )
```

```python
import functools

import jax
import jax.numpy as jnp
from jax import lax
from jax.experimental import pallas as pl
from jax.experimental.pallas import tpu as pltpu
from jax.sharding import PartitionSpec as P


def from_behind(value, axis, steps):
    count = lax.axis_size(axis)
    first, last = (max(0, -steps), min(count, count - steps))
    return lax.ppermute(value, axis, [(source, source + steps) for source in range(first, last)])


def local_segment(blocked, segment_coef, segment_bit):
    block_count, inner_rows, feature_count = blocked.shape
    stride_len = 2**segment_bit
    shaped = blocked.reshape(
        block_count // (2 * stride_len), 2, stride_len, inner_rows, feature_count
    )
    lower_part = shaped[:, 0].astype(jnp.float32)
    upper_part = shaped[:, 1].astype(jnp.float32)
    new_lower = segment_coef[0, 0] * lower_part + segment_coef[0, 1] * upper_part
    new_upper = segment_coef[1, 0] * upper_part + segment_coef[1, 1] * lower_part
    joined = jnp.stack([new_lower, new_upper], axis=1)
    return joined.reshape(block_count, inner_rows, feature_count).astype(jnp.bfloat16)


def local_back(grad_blocked, stored, segment_coef, segment_bit):
    block_count, inner_rows, feature_count = grad_blocked.shape
    stride_len = 2**segment_bit
    dshape = grad_blocked.reshape(
        block_count // (2 * stride_len), 2, stride_len, inner_rows, feature_count
    )
    zshape = stored.reshape(
        block_count // (2 * stride_len), 2, stride_len, inner_rows, feature_count
    )
    grad_lower = dshape[:, 0].astype(jnp.float32)
    grad_upper = dshape[:, 1].astype(jnp.float32)
    val_lower = zshape[:, 0].astype(jnp.float32)
    val_upper = zshape[:, 1].astype(jnp.float32)
    prev_lower = segment_coef[0, 0] * grad_lower + segment_coef[1, 1] * grad_upper
    prev_upper = segment_coef[1, 0] * grad_upper + segment_coef[0, 1] * grad_lower
    joined = jnp.stack([prev_lower, prev_upper], axis=1)
    prev = joined.reshape(block_count, inner_rows, feature_count).astype(jnp.bfloat16)
    axes_sum = (0, 1, 2)
    partial_value = jnp.stack(
        [
            jnp.stack(
                [
                    jnp.sum(grad_lower * val_lower, axis=axes_sum),
                    jnp.sum(grad_lower * val_upper, axis=axes_sum),
                ]
            ),
            jnp.stack(
                [
                    jnp.sum(grad_upper * val_upper, axis=axes_sum),
                    jnp.sum(grad_upper * val_lower, axis=axes_sum),
                ]
            ),
        ]
    )
    return (prev, partial_value)


def exchange_plan(inputs, grad_out, w_in, w_out, square_mix, twiddle_w):
    row_count, feature_count = inputs.shape
    seq_count = lax.axis_size("seq")
    segment_total = seq_count.bit_length() - 1
    projected = jnp.dot(inputs, w_in, preferred_element_type=jnp.float32)
    value = projected[:, :feature_count].astype(jnp.bfloat16)
    gate = projected[:, feature_count:].astype(jnp.bfloat16)
    first_segment = jnp.dot(square_mix, value, preferred_element_type=jnp.float32).astype(
        jnp.bfloat16
    )
    partials = [None] * segment_total
    columns = lax.all_to_all(first_segment, "seq", split_axis=0, concat_axis=0, tiled=True)
    blocked = columns.reshape(seq_count, row_count // seq_count, feature_count)
    stored = []
    for segment_bit in range(segment_total):
        stored.append(blocked)
        blocked = local_segment(blocked, twiddle_w[segment_bit], segment_bit)
    monarch = lax.all_to_all(
        blocked.reshape(row_count, feature_count), "seq", split_axis=0, concat_axis=0, tiled=True
    )
    hidden = (monarch.astype(jnp.float32) * gate.astype(jnp.float32)).astype(jnp.bfloat16)
    mixed_out = jnp.dot(hidden, w_out, preferred_element_type=jnp.float32).astype(jnp.bfloat16)
    d_hidden = lax.dot_general(
        grad_out, w_out, (((1,), (1,)), ((), ())), preferred_element_type=jnp.float32
    ).astype(jnp.bfloat16)
    wout_term = lax.dot_general(
        hidden, grad_out, (((0,), (0,)), ((), ())), preferred_element_type=jnp.float32
    )
    d_monarch = (d_hidden.astype(jnp.float32) * gate.astype(jnp.float32)).astype(jnp.bfloat16)
    d_gate = (d_hidden.astype(jnp.float32) * monarch.astype(jnp.float32)).astype(jnp.bfloat16)
    grad_columns = lax.all_to_all(d_monarch, "seq", split_axis=0, concat_axis=0, tiled=True)
    grad_blocked = grad_columns.reshape(seq_count, row_count // seq_count, feature_count)
    for segment_bit in range(segment_total - 1, -1, -1):
        grad_blocked, partials[segment_bit] = local_back(
            grad_blocked, stored[segment_bit], twiddle_w[segment_bit], segment_bit
        )
    d_first = lax.all_to_all(
        grad_blocked.reshape(row_count, feature_count),
        "seq",
        split_axis=0,
        concat_axis=0,
        tiled=True,
    )
    twiddle_grad = lax.psum(jnp.stack(partials), "seq")
    d_value = lax.dot_general(
        square_mix, d_first, (((0,), (0,)), ((), ())), preferred_element_type=jnp.float32
    ).astype(jnp.bfloat16)
    grad_square = lax.dot_general(
        d_first, value, (((1,), (1,)), ((), ())), preferred_element_type=jnp.float32
    )
    d_projected = jnp.concatenate([d_value, d_gate], axis=1)
    win_term = lax.dot_general(
        inputs, d_projected, (((0,), (0,)), ((), ())), preferred_element_type=jnp.float32
    )
    win_share, wout_share = (
        lax.psum_scatter(win_term, "seq", scatter_dimension=0, tiled=True),
        lax.psum_scatter(wout_term, "seq", scatter_dimension=0, tiled=True),
    )
    input_grad = lax.dot_general(
        d_projected, w_in, (((1,), (1,)), ((), ())), preferred_element_type=jnp.float32
    ).astype(jnp.bfloat16)
    handed = from_behind(input_grad, "pipe", -1)
    return mixed_out, handed, win_share, wout_share, grad_square, twiddle_grad


def chip_hops(hops):
    return [(2 * source + core, 2 * target + core) for source, target in hops for core in (0, 1)]


CORE_SWAP = [(index, index ^ 1) for index in range(8)]
INWARD = chip_hops([(0, 1), (3, 2)])
ACROSS = chip_hops([(1, 2), (2, 1)])
OUTWARD = chip_hops([(1, 0), (2, 3)])


def relay_back(outward):
    return [
        (8 * (section + 1) + source, 8 * section + target)
        for section in range(lax.axis_size("pipe") - 1)
        for source, target in (OUTWARD if outward else [(place, place) for place in range(2, 6)])
    ]


def hop(value, pairs):
    return lax.ppermute(value, "seq", pairs)


def dot(left, right):
    return jnp.dot(left, right, preferred_element_type=jnp.float32)


def dot_rows(left, right):
    return lax.dot_general(
        left, right, (((0,), (0,)), ((), ())), preferred_element_type=jnp.float32
    )


def dot_columns(left, right):
    return lax.dot_general(
        left, right, (((1,), (1,)), ((), ())), preferred_element_type=jnp.float32
    )


def narrow(value):
    return value.astype(jnp.bfloat16)


def wide(value):
    return value.astype(jnp.float32)


def coef_at(coef_ref, bit, side, term):
    return coef_ref[pl.ds(4 * bit + 2 * side + term, 1), :]


def cross(coef_ref, bit, side, own, other):
    return coef_at(coef_ref, bit, side, 0) * own + coef_at(coef_ref, bit, side, 1) * other


def cross_back(coef_ref, bit, side, own, other):
    return coef_at(coef_ref, bit, side, 0) * own + coef_at(coef_ref, bit, 1 - side, 1) * other


def pack_kernel(acts_ref, mix_ref, pack_ref):
    rows, width = acts_ref.shape
    depth = mix_ref.shape[1]
    piece = rows * depth // width
    pack_ref[pl.ds(0, rows), :] = acts_ref[...]
    for i in range(rows // piece):
        pack_ref[pl.ds(rows, piece), pl.ds(i * depth, depth)] = mix_ref[pl.ds(i * piece, piece), :]


def unpack_mix(pack_ref, rows):
    piece = pack_ref.shape[0] - rows
    return jnp.concatenate(
        [pack_ref[pl.ds(rows, piece), pl.ds(i * rows, rows)] for i in range(rows // piece)], axis=0
    )


def block_kernel(starts_ref, pack_ref, weight_ref, columns_ref, mixed_ref, gate_ref, *refs):
    rows, width = gate_ref.shape
    seg0, value = (refs[:2], ()) if refs[0].shape[1] < width else (refs[:1], refs[1:])
    half, share = width // 2, width // 8
    acts = pack_ref[pl.ds(0, rows), :]
    mix = unpack_mix(pack_ref, rows)
    for i in range(4):
        product = narrow(dot(acts, weight_ref[:, pl.ds(i * half, half)]))
        if i < 2:
            segment = narrow(dot(mix, product))
            if len(seg0) == 2:
                seg0[i][...] = segment
            else:
                seg0[0][:, pl.ds(i * half, half)] = segment
            if value:
                value[0][:, pl.ds(i * half, half)] = product
        else:
            gate_ref[:, pl.ds((i - 2) * half, half)] = product
    for j in range(4):
        start = pl.multiple_of(starts_ref[j], share)
        columns_ref[:, pl.ds(j * share, share)] = pack_ref[pl.ds(0, rows), pl.ds(start, share)]
    mixed_ref[...] = narrow(dot(mix, columns_ref[...]))


def d_hidden_kernel(weight_ref, *refs):
    for cotan_ref, out_ref in zip(refs[: len(refs) // 2], refs[len(refs) // 2 :]):
        out_ref[...] = narrow(dot_columns(cotan_ref[...], weight_ref[...]))


def early_grads_kernel(*refs):
    columns, d_gate_ref, hidden_ref, cotans = refs[0:4], refs[4], refs[5], refs[6:10]
    given_refs, kept_ref = refs[10:14], refs[14]
    half = kept_ref.shape[0] // 2
    d_gates = [d_gate_ref.at[k] for k in range(4)]
    split_grad(columns, d_gates, given_refs[0:2], kept_ref.at[pl.ds(0, half), :])
    hiddens = [hidden_ref.at[k] for k in range(4)]
    split_grad(hiddens, cotans, given_refs[2:4], kept_ref.at[pl.ds(half, half), :])


def split_grad(lefts, rights, given_refs, kept_ref):
    half = kept_ref.shape[0]
    for part in range(2):
        total = 0.0
        for left, right in zip(lefts, rights):
            total += dot_rows(left[:, pl.ds(part * half, half)], right[...])
        if part == 0:
            for i, ref in enumerate(given_refs):
                size = ref.shape[0]
                ref[...] = narrow(total[i * size : (i + 1) * size])
        else:
            kept_ref[...] = total


def value_grads_kernel(d_seg0_ref, *refs):
    values, given_refs, kept_ref = refs[4:6], refs[6:8], refs[8]
    split_grad(refs[0:4], [d_seg0_ref.at[k] for k in range(4)], given_refs, kept_ref)
    for k in range(2):
        refs[9 + k][...] = dot_columns(d_seg0_ref[k], values[k][...])


def sums_kernel(kept_ref, *refs):
    out_ref = refs[-1]
    share = kept_ref.shape[1] // 8
    terms = kept_ref.shape[0] // (2 * share)
    got, extra = refs[: 2 * terms], refs[2 * terms : -1]
    for i in range(terms):
        there = kept_ref[pl.ds((2 * i + 1) * share, share), :]
        out_ref[pl.ds(i * share, share), :] = narrow(there + wide(got[2 * i + 1][...]))
    for ref in extra:
        depth = ref.shape[1]
        piece = out_ref.shape[0] - terms * share
        for i in range(ref.shape[0] // piece):
            out_ref[pl.ds(terms * share, piece), pl.ds(i * depth, depth)] = narrow(
                ref[pl.ds(i * piece, piece), :]
            )


def own_kernel(d_seg0_ref, d_gate_ref, weight_ref, *refs):
    packs, d_acts = refs[0:2], refs[2:4]
    rows, width = d_acts[0].shape
    for k in range(2):
        d_value = narrow(dot_rows(unpack_mix(packs[k], rows), d_seg0_ref[k]))
        d_acts[k][...] = narrow(
            dot_columns(d_value, weight_ref[:, pl.ds(0, width)])
            + dot_columns(d_gate_ref[k], weight_ref[:, pl.ds(width, width)])
        )


def mixed_kernel(hidden_ref, weight_ref, *outs):
    for k in range(2):
        outs[k][...] = narrow(dot(hidden_ref[k], weight_ref[...]))


def joined_far(refs):
    far = jnp.concatenate([refs[3][...], refs[4][...]], axis=1)
    return [refs[0][...], refs[1][...], far, refs[2][...]]


def forward_kernel(starts_ref, coef_ref, *refs):
    seg0, swapped = joined_far(refs[0:5]), joined_far(refs[5:10])
    gates = refs[10:14]
    seg1_out, seg2_out, hidden_out, columns_out, held = refs[14:19]
    share = coef_ref.shape[1] // 8
    first = [cross(coef_ref, 0, 0, seg0[k], swapped[k]) for k in range(4)]
    for k in range(2):
        seg1_out[k] = first[k]
    second = [cross(coef_ref, 1, k & 1, first[k], first[k ^ 1]) for k in range(4)]
    for k in range(4):
        seg2_out[k] = second[k]
    for k in range(4):
        hidden = cross(coef_ref, 2, k >> 1, second[k], second[k ^ 2]) * gates[k][...]
        held[k] = hidden
        if k < 2:
            hidden_out[k] = hidden
    for k in range(4):
        for j in range(4):
            start = pl.multiple_of(starts_ref[j], share)
            columns_out[k, :, pl.ds(j * share, share)] = held[k, :, pl.ds(start, share)]


def row_sums(value, row):
    shape = (8, value.shape[0])
    chosen = lax.broadcasted_iota(jnp.int32, shape, 0) == row
    return dot(jnp.where(chosen, 1.0, 0.0).astype(value.dtype), value)


def backward_kernel(coef_ref, *refs):
    d_hidden = refs[0:4]
    gates = refs[4:8]
    seg1_ref, seg2_ref = refs[8:10]
    d_gate_out, d_seg1_out, partial_out = refs[10], refs[11:15], refs[15]

    @pl.when(pl.program_id(0) == 0)
    def _():
        partial_out[...] = jnp.zeros_like(partial_out)

    third = []
    for k in range(4):
        grad = d_hidden[k][...]
        d_gate_out[k] = grad * cross(coef_ref, 2, k >> 1, seg2_ref[k], seg2_ref[k ^ 2])
        third.append(grad * gates[k][...])
    for k in range(2):
        partial_out[...] += row_sums(third[k] * seg2_ref[k], 4)
        partial_out[...] += row_sums(third[k] * seg2_ref[k ^ 2], 5)
    second = [cross_back(coef_ref, 2, k >> 1, third[k], third[k ^ 2]) for k in range(4)]
    for k in range(2):
        partial_out[...] += row_sums(second[k] * seg1_ref[k], 2 * k)
        partial_out[...] += row_sums(second[k] * seg1_ref[k ^ 1], 2 * k + 1)
    for k in range(4):
        d_seg1_out[k][...] = cross_back(coef_ref, 1, k & 1, second[k], second[k ^ 1])


def first_bit_kernel(coef_ref, *refs):
    d_seg1, d_swapped = refs[0:4], refs[4:8]
    seg0 = refs[8:10]
    swapped = refs[10:12]
    d_seg0_out, partial_out = refs[12:14]

    @pl.when(pl.program_id(0) == 0)
    def _():
        partial_out[...] = jnp.zeros_like(partial_out)

    for k in range(4):
        own, other = d_seg1[k][...], d_swapped[k][...]
        d_seg0 = cross_back(coef_ref, 0, 0, own, other)
        d_seg0_out[k] = d_seg0
        if k < 2:
            partial_out[...] += row_sums(own * seg0[k][...], 0)
            partial_out[...] += row_sums(own * swapped[k][...], 1)


TILE = 64


def tile(columns, column_at=0, row_at=0):
    return pl.BlockSpec((TILE, columns), lambda i: (i + row_at, column_at))


def stacked(count, columns, row_at=0):
    return pl.BlockSpec((count, TILE, columns), lambda i: (0, i + row_at, 0))


def whole(*shape):
    return pl.BlockSpec(shape, lambda i: (0,) * len(shape))


def shape_of(kind, *shape):
    return jax.ShapeDtypeStruct(shape, kind)


def in_hbm(kind, *shape):
    return pltpu.HBM(shape, kind)


def kernel_call(kernel, name, work=1, room=16, **settings):
    return pl.pallas_call(
        kernel,
        cost_estimate=pl.CostEstimate(flops=work, bytes_accessed=1, transcendentals=0),
        compiler_params=pltpu.CompilerParams(vmem_limit_bytes=room * 2**20),
        name=name,
        **settings,
    )


def in_place(kernel, name, operands, *outs, work=1, scalars=0, room=16):
    local = pl.BlockSpec(memory_space=pltpu.VMEM)
    return kernel_call(
        kernel,
        name,
        work,
        room,
        in_specs=[pl.BlockSpec(memory_space=pltpu.SMEM)] * scalars
        + [local] * (len(operands) - scalars),
        out_specs=[local] * len(outs),
        out_shape=list(outs),
    )(*operands)


def after(value, *earlier):
    return lax.optimization_barrier((value, *earlier))[0]


def relay_plan(inputs, grad_out, w_in, w_out, mix, twiddle_w):
    rows, width = inputs.shape
    share = width // 8
    bf16, f32 = jnp.bfloat16, jnp.float32
    place = lax.axis_index("seq")
    chip, core = place // 2, place % 2
    inner = (chip == 1) | (chip == 2)
    flips = (core, chip & 1, chip >> 1)
    scalar = pl.BlockSpec(memory_space=pltpu.SMEM)

    starts = jnp.stack(
        [
            (2 * (chip ^ chip_bit) + (core ^ core_bit)) * share
            for core_bit in (1, 0)
            for chip_bit in (0, 1)
        ]
    ).astype(jnp.int32)

    full, full_hbm = shape_of(bf16, rows, width), in_hbm(bf16, rows, width)
    narrow_hbm = in_hbm(bf16, rows, width // 2)
    packed_rows = rows + mix.size // width
    (pack,) = in_place(
        pack_kernel, "pack", [inputs, mix], in_hbm(bf16, packed_rows, width), room=60
    )

    def block(k, packed, work=1):
        return in_place(
            block_kernel,
            f"block_{k}",
            [starts, packed, w_in],
            *([narrow_hbm] * 2 + [full_hbm]),
            *([narrow_hbm] * 2 if k == 2 else [full_hbm] * (1 + (k < 2))),
            work=work,
            scalars=1,
        )

    outer_pack, across_pack = hop(pack, INWARD), hop(pack, ACROSS)
    own = block(0, pack, 4 * rows * width * width)
    (d_hidden_own,) = in_place(
        d_hidden_kernel, "d_hidden", [w_out, grad_out], full, work=2 * rows * width * width
    )
    far_pack = hop(after(outer_pack, own[0], d_hidden_own), ACROSS)
    outer_cotan = hop(after(grad_out, outer_pack), INWARD)
    across_cotan = hop(after(grad_out, outer_pack), ACROSS)
    far_cotan = hop(outer_cotan, ACROSS)
    outer = block(1, outer_pack)
    across = block(3, after(across_pack, outer[0]))
    far = block(2, after(far_pack, outer_cotan, across[0]))

    coefs = jnp.concatenate(
        [
            jnp.where(flips[bit] == 1, twiddle_w[bit][::-1], twiddle_w[bit]).reshape(4, width)
            for bit in range(3)
        ]
        + [jnp.zeros((4, width), jnp.float32)]
    ).astype(bf16)
    blocks = [own, outer, far, across]
    gates = [part[2] for part in blocks]
    seg0 = [own[3], outer[3], across[3], far[3], far[4]]
    swapped = [hop(part, CORE_SWAP) for part in seg0]
    seg1, seg2, hidden, hidden_columns = kernel_call(
        forward_kernel,
        "forward_segments",
        room=60,
        grid=(rows // TILE,),
        in_specs=[scalar, whole(16, width)]
        + ([tile(width)] * 3 + [tile(width // 2)] * 2) * 2
        + [tile(width)] * 4,
        out_specs=[
            stacked(2, width),
            stacked(4, width),
            stacked(2, width),
            stacked(4, width // 2),
        ],
        out_shape=[
            shape_of(bf16, 2, rows, width),
            shape_of(bf16, 4, rows, width),
            shape_of(bf16, 2, rows, width),
            shape_of(bf16, 4, rows, width // 2),
        ],
        scratch_shapes=[pltpu.VMEM((4, TILE, width), bf16)],
    )(starts, coefs, *seg0, after(swapped[0], across_cotan), *swapped[1:], *gates)
    own_mixed, outer_mixed = in_place(
        mixed_kernel, "mixed", [hidden, w_out], full, full
    )
    sent_mixed = hop(outer_mixed, OUTWARD)

    d_hidden_outer, d_hidden_across = in_place(
        d_hidden_kernel,
        "d_hidden",
        [w_out, after(outer_cotan, outer_mixed), across_cotan],
        *[full] * 2,
    )
    (d_hidden_far,) = in_place(
        d_hidden_kernel, "d_hidden", [w_out, after(far_cotan, d_hidden_outer)], full
    )
    d_hidden = [d_hidden_own, d_hidden_outer, d_hidden_far, d_hidden_across]
    d_gate, *d_seg1, later_part = kernel_call(
        backward_kernel,
        "backward_segments",
        grid=(rows // TILE,),
        in_specs=[whole(16, width)]
        + [tile(width)] * 8
        + [stacked(2, width), stacked(4, width)],
        out_specs=[stacked(4, width)] + [tile(width)] * 4 + [whole(8, width)],
        out_shape=[shape_of(bf16, 4, rows, width)] + [full] * 4 + [shape_of(f32, 8, width)],
    )(coefs, *d_hidden, *gates, seg1, seg2)
    d_swapped = [hop(part, CORE_SWAP) for part in d_seg1]

    *early_given, early_kept = in_place(
        early_grads_kernel,
        "early_grads",
        [part[0] for part in blocks]
        + [d_gate, hidden_columns, grad_out, outer_cotan, far_cotan, across_cotan],
        *[shape_of(bf16, share, width)] * 4,
        shape_of(f32, 4 * share, width),
    )
    early_got = [hop(part, CORE_SWAP) for part in early_given]
    (early_sums,) = in_place(
        sums_kernel, "early_sums", [after(early_kept, sent_mixed, *d_swapped), *early_got], shape_of(bf16, 2 * share, width)
    )
    sent_early = hop(early_sums, OUTWARD)
    d_seg0, first_part = kernel_call(
        first_bit_kernel,
        "first_segment_grad",
        grid=(rows // TILE,),
        in_specs=[whole(16, width)] + [tile(width)] * 12,
        out_specs=[stacked(4, width), whole(8, width)],
        out_shape=[shape_of(bf16, 4, rows, width), shape_of(f32, 8, width)],
    )(coefs, *d_seg1, after(d_swapped[0], early_sums), *d_swapped[1:], *seg0[:2], *swapped[:2])
    *late_given, late_kept, own_square, outer_square = in_place(
        value_grads_kernel,
        "value_grads",
        [d_seg0] + [part[1] for part in blocks] + [own[4], outer[4]],
        *[shape_of(bf16, share, width)] * 2,
        in_hbm(f32, 2 * share, width),
        in_hbm(f32, rows, rows),
        in_hbm(f32, rows, rows),
    )
    late_got = [hop(part, CORE_SWAP) for part in late_given]
    (late_sums,) = in_place(
        sums_kernel,
        "late_sums",
        [late_kept, *late_got, outer_square],
        shape_of(bf16, share + rows * rows // width, width),
    )
    sent_late = hop(late_sums, OUTWARD)
    own_d_acts, outer_d_acts = in_place(
        own_kernel,
        "own_grads",
        [after(d_seg0, late_sums, sent_early), d_gate, w_in, pack, outer_pack],
        full,
        full,
    )
    outer_handed = lax.ppermute(outer_d_acts, ("pipe", "seq"), relay_back(True))
    own_handed = lax.ppermute(own_d_acts, ("pipe", "seq"), relay_back(False))

    def one_side(pair_terms, flip):
        empty = jnp.zeros_like(pair_terms)
        return jnp.where(
            flip == 1, jnp.stack([empty, pair_terms]), jnp.stack([pair_terms, empty])
        )

    first_terms, later_terms = lax.optimization_barrier(
        (first_part[:2], later_part, outer_d_acts, late_sums)
    )[:2]
    both = later_terms[:4].reshape(2, 2, width)
    terms = jnp.stack(
        [
            one_side(first_terms, flips[0]),
            jnp.where(flips[1] == 1, both[::-1], both),
            one_side(later_terms[4:6], flips[2]),
        ]
    )
    terms = terms + hop(terms, CORE_SWAP)
    terms = terms + hop(terms, ACROSS)
    twiddle_grad = jnp.where(inner, terms, hop(after(terms, sent_late), OUTWARD))

    mixed_out = jnp.where(inner, own_mixed, after(sent_mixed, outer_d_acts))
    sent_early = after(sent_early, outer_d_acts)

    def share_of(kept, got, sent, at):
        mine = kept[2 * at * share : (2 * at + 1) * share] + wide(got[2 * at])
        return jnp.where(inner, mine, wide(sent[at * share : (at + 1) * share]))

    win_share = jnp.concatenate(
        [share_of(late_kept, late_got, sent_late, 0), share_of(early_kept, early_got, sent_early, 0)],
        axis=1,
    )
    wout_share = share_of(early_kept, early_got, sent_early, 1)
    sent_square = jnp.concatenate(
        [sent_late[share:, i * rows : (i + 1) * rows] for i in range(width // rows)]
    )
    grad_square = jnp.where(inner, own_square, wide(sent_square))
    handed = jnp.where(inner, own_handed, outer_handed)
    return mixed_out, handed, win_share, wout_share, grad_square, twiddle_grad


def on_device(*arguments):
    plan = relay_plan if lax.axis_size("seq") == 8 else exchange_plan
    return tuple(result[None] for result in plan(*(part[0] for part in arguments)))


def solution(mesh):
    in_specs = (
        P("pipe", "seq", None),
        P("pipe", "seq", None),
        P("pipe", None, None),
        P("pipe", None, None),
        P("pipe", "seq", None),
        P("pipe", None, None, None, None),
    )
    out_specs = (
        P("pipe", "seq", None),
        P("pipe", "seq", None),
        P("pipe", "seq", None),
        P("pipe", "seq", None),
        P("pipe", "seq", None),
        P("pipe", None, None, None, None),
    )
    return jax.shard_map(
        on_device, mesh=mesh, in_specs=in_specs, out_specs=out_specs, check_vma=False
    )
```

```python
import functools

import jax
import jax.numpy as jnp
from jax import lax
from jax.experimental import pallas as pl
from jax.experimental.pallas import tpu as pltpu
from jax.sharding import PartitionSpec as P


def from_behind(value, axis, steps):
    count = lax.axis_size(axis)
    first, last = (max(0, -steps), min(count, count - steps))
    return lax.ppermute(value, axis, [(source, source + steps) for source in range(first, last)])


def local_segment(blocked, segment_coef, segment_bit):
    block_count, inner_rows, feature_count = blocked.shape
    stride_len = 2**segment_bit
    shaped = blocked.reshape(
        block_count // (2 * stride_len), 2, stride_len, inner_rows, feature_count
    )
    lower_part = shaped[:, 0].astype(jnp.float32)
    upper_part = shaped[:, 1].astype(jnp.float32)
    new_lower = segment_coef[0, 0] * lower_part + segment_coef[0, 1] * upper_part
    new_upper = segment_coef[1, 0] * upper_part + segment_coef[1, 1] * lower_part
    joined = jnp.stack([new_lower, new_upper], axis=1)
    return joined.reshape(block_count, inner_rows, feature_count).astype(jnp.bfloat16)


def local_back(grad_blocked, stored, segment_coef, segment_bit):
    block_count, inner_rows, feature_count = grad_blocked.shape
    stride_len = 2**segment_bit
    dshape = grad_blocked.reshape(
        block_count // (2 * stride_len), 2, stride_len, inner_rows, feature_count
    )
    zshape = stored.reshape(
        block_count // (2 * stride_len), 2, stride_len, inner_rows, feature_count
    )
    grad_lower = dshape[:, 0].astype(jnp.float32)
    grad_upper = dshape[:, 1].astype(jnp.float32)
    val_lower = zshape[:, 0].astype(jnp.float32)
    val_upper = zshape[:, 1].astype(jnp.float32)
    prev_lower = segment_coef[0, 0] * grad_lower + segment_coef[1, 1] * grad_upper
    prev_upper = segment_coef[1, 0] * grad_upper + segment_coef[0, 1] * grad_lower
    joined = jnp.stack([prev_lower, prev_upper], axis=1)
    prev = joined.reshape(block_count, inner_rows, feature_count).astype(jnp.bfloat16)
    axes_sum = (0, 1, 2)
    partial_value = jnp.stack(
        [
            jnp.stack(
                [
                    jnp.sum(grad_lower * val_lower, axis=axes_sum),
                    jnp.sum(grad_lower * val_upper, axis=axes_sum),
                ]
            ),
            jnp.stack(
                [
                    jnp.sum(grad_upper * val_upper, axis=axes_sum),
                    jnp.sum(grad_upper * val_lower, axis=axes_sum),
                ]
            ),
        ]
    )
    return (prev, partial_value)


def exchange_plan(inputs, grad_out, w_in, w_out, square_mix, twiddle_w):
    row_count, feature_count = inputs.shape
    seq_count = lax.axis_size("seq")
    segment_total = seq_count.bit_length() - 1
    projected = jnp.dot(inputs, w_in, preferred_element_type=jnp.float32)
    value = projected[:, :feature_count].astype(jnp.bfloat16)
    gate = projected[:, feature_count:].astype(jnp.bfloat16)
    first_segment = jnp.dot(square_mix, value, preferred_element_type=jnp.float32).astype(
        jnp.bfloat16
    )
    partials = [None] * segment_total
    columns = lax.all_to_all(first_segment, "seq", split_axis=0, concat_axis=0, tiled=True)
    blocked = columns.reshape(seq_count, row_count // seq_count, feature_count)
    stored = []
    for segment_bit in range(segment_total):
        stored.append(blocked)
        blocked = local_segment(blocked, twiddle_w[segment_bit], segment_bit)
    monarch = lax.all_to_all(
        blocked.reshape(row_count, feature_count), "seq", split_axis=0, concat_axis=0, tiled=True
    )
    hidden = (monarch.astype(jnp.float32) * gate.astype(jnp.float32)).astype(jnp.bfloat16)
    mixed_out = jnp.dot(hidden, w_out, preferred_element_type=jnp.float32).astype(jnp.bfloat16)
    d_hidden = lax.dot_general(
        grad_out, w_out, (((1,), (1,)), ((), ())), preferred_element_type=jnp.float32
    ).astype(jnp.bfloat16)
    wout_term = lax.dot_general(
        hidden, grad_out, (((0,), (0,)), ((), ())), preferred_element_type=jnp.float32
    )
    d_monarch = (d_hidden.astype(jnp.float32) * gate.astype(jnp.float32)).astype(jnp.bfloat16)
    d_gate = (d_hidden.astype(jnp.float32) * monarch.astype(jnp.float32)).astype(jnp.bfloat16)
    grad_columns = lax.all_to_all(d_monarch, "seq", split_axis=0, concat_axis=0, tiled=True)
    grad_blocked = grad_columns.reshape(seq_count, row_count // seq_count, feature_count)
    for segment_bit in range(segment_total - 1, -1, -1):
        grad_blocked, partials[segment_bit] = local_back(
            grad_blocked, stored[segment_bit], twiddle_w[segment_bit], segment_bit
        )
    d_first = lax.all_to_all(
        grad_blocked.reshape(row_count, feature_count),
        "seq",
        split_axis=0,
        concat_axis=0,
        tiled=True,
    )
    twiddle_grad = lax.psum(jnp.stack(partials), "seq")
    d_value = lax.dot_general(
        square_mix, d_first, (((0,), (0,)), ((), ())), preferred_element_type=jnp.float32
    ).astype(jnp.bfloat16)
    grad_square = lax.dot_general(
        d_first, value, (((1,), (1,)), ((), ())), preferred_element_type=jnp.float32
    )
    d_projected = jnp.concatenate([d_value, d_gate], axis=1)
    win_term = lax.dot_general(
        inputs, d_projected, (((0,), (0,)), ((), ())), preferred_element_type=jnp.float32
    )
    win_share, wout_share = (
        lax.psum_scatter(win_term, "seq", scatter_dimension=0, tiled=True),
        lax.psum_scatter(wout_term, "seq", scatter_dimension=0, tiled=True),
    )
    input_grad = lax.dot_general(
        d_projected, w_in, (((1,), (1,)), ((), ())), preferred_element_type=jnp.float32
    ).astype(jnp.bfloat16)
    handed = from_behind(input_grad, "pipe", -1)
    return mixed_out, handed, win_share, wout_share, grad_square, twiddle_grad


def chip_hops(hops):
    return [(2 * source + core, 2 * target + core) for source, target in hops for core in (0, 1)]


CORE_SWAP = [(index, index ^ 1) for index in range(8)]
INWARD = chip_hops([(0, 1), (3, 2)])
ACROSS = chip_hops([(1, 2), (2, 1)])
OUTWARD = chip_hops([(1, 0), (2, 3)])


def relay_back(outward):
    return [
        (8 * (section + 1) + source, 8 * section + target)
        for section in range(lax.axis_size("pipe") - 1)
        for source, target in (OUTWARD if outward else [(place, place) for place in range(2, 6)])
    ]


def hop(value, pairs):
    return lax.ppermute(value, "seq", pairs)


def dot(left, right):
    return jnp.dot(left, right, preferred_element_type=jnp.float32)


def dot_rows(left, right):
    return lax.dot_general(
        left, right, (((0,), (0,)), ((), ())), preferred_element_type=jnp.float32
    )


def dot_columns(left, right):
    return lax.dot_general(
        left, right, (((1,), (1,)), ((), ())), preferred_element_type=jnp.float32
    )


def narrow(value):
    return value.astype(jnp.bfloat16)


def wide(value):
    return value.astype(jnp.float32)


def coef_at(coef_ref, bit, side, term):
    return coef_ref[pl.ds(4 * bit + 2 * side + term, 1), :]


def cross(coef_ref, bit, side, own, other):
    return coef_at(coef_ref, bit, side, 0) * own + coef_at(coef_ref, bit, side, 1) * other


def cross_back(coef_ref, bit, side, own, other):
    return coef_at(coef_ref, bit, side, 0) * own + coef_at(coef_ref, bit, 1 - side, 1) * other


def pack_kernel(acts_ref, mix_ref, pack_ref):
    rows, width = acts_ref.shape
    depth = mix_ref.shape[1]
    piece = rows * depth // width
    pack_ref[pl.ds(0, rows), :] = acts_ref[...]
    for i in range(rows // piece):
        pack_ref[pl.ds(rows, piece), pl.ds(i * depth, depth)] = mix_ref[pl.ds(i * piece, piece), :]


def unpack_mix(pack_ref, rows):
    piece = pack_ref.shape[0] - rows
    return jnp.concatenate(
        [pack_ref[pl.ds(rows, piece), pl.ds(i * rows, rows)] for i in range(rows // piece)], axis=0
    )


def block_kernel(starts_ref, pack_ref, weight_ref, columns_ref, mixed_ref, gate_ref, *refs):
    rows, width = gate_ref.shape
    seg0, value = (refs[:2], ()) if refs[0].shape[1] < width else (refs[:1], refs[1:])
    half, share = width // 2, width // 8
    acts = pack_ref[pl.ds(0, rows), :]
    mix = unpack_mix(pack_ref, rows)
    for i in range(4):
        product = narrow(dot(acts, weight_ref[:, pl.ds(i * half, half)]))
        if i < 2:
            segment = narrow(dot(mix, product))
            if len(seg0) == 2:
                seg0[i][...] = segment
            else:
                seg0[0][:, pl.ds(i * half, half)] = segment
            if value:
                value[0][:, pl.ds(i * half, half)] = product
        else:
            gate_ref[:, pl.ds((i - 2) * half, half)] = product
    for j in range(4):
        start = pl.multiple_of(starts_ref[j], share)
        columns_ref[:, pl.ds(j * share, share)] = pack_ref[pl.ds(0, rows), pl.ds(start, share)]
    mixed_ref[...] = narrow(dot(mix, columns_ref[...]))


def d_hidden_kernel(weight_ref, *refs):
    for cotan_ref, out_ref in zip(refs[: len(refs) // 2], refs[len(refs) // 2 :]):
        out_ref[...] = narrow(dot_columns(cotan_ref[...], weight_ref[...]))


def early_grads_kernel(*refs):
    columns, d_gate_ref, hidden_ref, cotans = refs[0:4], refs[4], refs[5], refs[6:10]
    given_refs, kept_ref = refs[10:14], refs[14]
    half = kept_ref.shape[0] // 2
    d_gates = [d_gate_ref.at[k] for k in range(4)]
    split_grad(columns, d_gates, given_refs[0:2], [kept_ref.at[pl.ds(0, half), :]])
    hiddens = [hidden_ref.at[k] for k in range(4)]
    split_grad(hiddens, cotans, given_refs[2:4], [kept_ref.at[pl.ds(half, half), :]])


def split_grad(lefts, rights, given_refs, kept_refs):
    half = sum(ref.shape[0] for ref in kept_refs)
    for part in range(2):
        total = 0.0
        for left, right in zip(lefts, rights):
            total += dot_rows(left[:, pl.ds(part * half, half)], right[...])
        if part == 0:
            for i, ref in enumerate(given_refs):
                size = ref.shape[0]
                ref[...] = narrow(total[i * size : (i + 1) * size])
        else:
            for i, ref in enumerate(kept_refs):
                size = ref.shape[0]
                ref[...] = total[i * size : (i + 1) * size]


def value_grads_kernel(d_seg0_ref, *refs):
    values, given_refs, kept_refs = refs[4:6], refs[6:8], refs[8:10]
    split_grad(refs[0:4], [d_seg0_ref.at[k] for k in range(4)], given_refs, kept_refs)
    for k in range(2):
        refs[10 + k][...] = dot_columns(d_seg0_ref[k], values[k][...])


def early_sums_kernel(kept_ref, *refs):
    got, out_ref = refs[:4], refs[4]
    share = out_ref.shape[0] // 2
    for i in range(2):
        there = kept_ref[pl.ds((2 * i + 1) * share, share), :]
        out_ref[pl.ds(i * share, share), :] = narrow(there + wide(got[2 * i + 1][...]))


def late_sums_kernel(there_ref, got_ref, square_ref, out_ref):
    share = there_ref.shape[0]
    out_ref[pl.ds(0, share), :] = narrow(there_ref[...] + wide(got_ref[...]))
    depth = square_ref.shape[1]
    piece = out_ref.shape[0] - share
    for i in range(square_ref.shape[0] // piece):
        out_ref[pl.ds(share, piece), pl.ds(i * depth, depth)] = narrow(
            square_ref[pl.ds(i * piece, piece), :]
        )


def own_kernel(d_seg0_ref, d_gate_ref, weight_ref, *refs):
    packs, d_acts = refs[0:2], refs[2:4]
    rows, width = d_acts[0].shape
    for k in range(2):
        d_value = narrow(dot_rows(unpack_mix(packs[k], rows), d_seg0_ref[k]))
        d_acts[k][...] = narrow(
            dot_columns(d_value, weight_ref[:, pl.ds(0, width)])
            + dot_columns(d_gate_ref[k], weight_ref[:, pl.ds(width, width)])
        )


def mixed_kernel(hidden_ref, weight_ref, *outs):
    for k in range(2):
        outs[k][...] = narrow(dot(hidden_ref[k], weight_ref[...]))


def joined_far(refs):
    far = jnp.concatenate([refs[3][...], refs[4][...]], axis=1)
    return [refs[0][...], refs[1][...], far, refs[2][...]]


def forward_kernel(starts_ref, coef_ref, *refs):
    seg0, swapped = joined_far(refs[0:5]), joined_far(refs[5:10])
    gates = refs[10:14]
    seg1_out, seg2_out, hidden_out, columns_out, held = refs[14:19]
    share = coef_ref.shape[1] // 8
    first = [cross(coef_ref, 0, 0, seg0[k], swapped[k]) for k in range(4)]
    for k in range(2):
        seg1_out[k] = first[k]
    second = [cross(coef_ref, 1, k & 1, first[k], first[k ^ 1]) for k in range(4)]
    for k in range(4):
        seg2_out[k] = second[k]
    for k in range(4):
        hidden = cross(coef_ref, 2, k >> 1, second[k], second[k ^ 2]) * gates[k][...]
        held[k] = hidden
        if k < 2:
            hidden_out[k] = hidden
    for k in range(4):
        for j in range(4):
            start = pl.multiple_of(starts_ref[j], share)
            columns_out[k, :, pl.ds(j * share, share)] = held[k, :, pl.ds(start, share)]


def row_sums(value, row):
    shape = (8, value.shape[0])
    chosen = lax.broadcasted_iota(jnp.int32, shape, 0) == row
    return dot(jnp.where(chosen, 1.0, 0.0).astype(value.dtype), value)


def backward_kernel(coef_ref, *refs):
    d_hidden = refs[0:4]
    gates = refs[4:8]
    seg1_ref, seg2_ref = refs[8:10]
    d_gate_out, d_seg1_out, partial_out = refs[10], refs[11:15], refs[15]

    @pl.when(pl.program_id(0) == 0)
    def _():
        partial_out[...] = jnp.zeros_like(partial_out)

    third = []
    for k in range(4):
        grad = d_hidden[k][...]
        d_gate_out[k] = grad * cross(coef_ref, 2, k >> 1, seg2_ref[k], seg2_ref[k ^ 2])
        third.append(grad * gates[k][...])
    for k in range(2):
        partial_out[...] += row_sums(third[k] * seg2_ref[k], 4)
        partial_out[...] += row_sums(third[k] * seg2_ref[k ^ 2], 5)
    second = [cross_back(coef_ref, 2, k >> 1, third[k], third[k ^ 2]) for k in range(4)]
    for k in range(2):
        partial_out[...] += row_sums(second[k] * seg1_ref[k], 2 * k)
        partial_out[...] += row_sums(second[k] * seg1_ref[k ^ 1], 2 * k + 1)
    for k in range(4):
        d_seg1_out[k][...] = cross_back(coef_ref, 1, k & 1, second[k], second[k ^ 1])


def first_bit_kernel(coef_ref, *refs):
    d_seg1, d_swapped = refs[0:4], refs[4:8]
    seg0 = refs[8:10]
    swapped = refs[10:12]
    d_seg0_out, partial_out = refs[12:14]

    @pl.when(pl.program_id(0) == 0)
    def _():
        partial_out[...] = jnp.zeros_like(partial_out)

    for k in range(4):
        own, other = d_seg1[k][...], d_swapped[k][...]
        d_seg0 = cross_back(coef_ref, 0, 0, own, other)
        d_seg0_out[k] = d_seg0
        if k < 2:
            partial_out[...] += row_sums(own * seg0[k][...], 0)
            partial_out[...] += row_sums(own * swapped[k][...], 1)


TILE = 128


def tile(columns, column_at=0, row_at=0):
    return pl.BlockSpec((TILE, columns), lambda i: (i + row_at, column_at))


def stacked(count, columns, row_at=0):
    return pl.BlockSpec((count, TILE, columns), lambda i: (0, i + row_at, 0))


def whole(*shape):
    return pl.BlockSpec(shape, lambda i: (0,) * len(shape))


def shape_of(kind, *shape):
    return jax.ShapeDtypeStruct(shape, kind)


def in_hbm(kind, *shape):
    return pltpu.HBM(shape, kind)


def kernel_call(kernel, name, work=1, room=16, **settings):
    return pl.pallas_call(
        kernel,
        cost_estimate=pl.CostEstimate(flops=work, bytes_accessed=1, transcendentals=0),
        compiler_params=pltpu.CompilerParams(vmem_limit_bytes=room * 2**20),
        name=name,
        **settings,
    )


def in_place(kernel, name, operands, *outs, work=1, scalars=0, room=16):
    local = pl.BlockSpec(memory_space=pltpu.VMEM)
    return kernel_call(
        kernel,
        name,
        work,
        room,
        in_specs=[pl.BlockSpec(memory_space=pltpu.SMEM)] * scalars
        + [local] * (len(operands) - scalars),
        out_specs=[local] * len(outs),
        out_shape=list(outs),
    )(*operands)


def after(value, *earlier):
    return lax.optimization_barrier((value, *earlier))[0]


def relay_plan(inputs, grad_out, w_in, w_out, mix, twiddle_w):
    rows, width = inputs.shape
    share = width // 8
    bf16, f32 = jnp.bfloat16, jnp.float32
    place = lax.axis_index("seq")
    chip, core = place // 2, place % 2
    inner = (chip == 1) | (chip == 2)
    flips = (core, chip & 1, chip >> 1)
    scalar = pl.BlockSpec(memory_space=pltpu.SMEM)

    starts = jnp.stack(
        [
            (2 * (chip ^ chip_bit) + (core ^ core_bit)) * share
            for core_bit in (1, 0)
            for chip_bit in (0, 1)
        ]
    ).astype(jnp.int32)

    coefs = jnp.concatenate(
        [
            jnp.where(flips[bit] == 1, twiddle_w[bit][::-1], twiddle_w[bit]).reshape(4, width)
            for bit in range(3)
        ]
        + [jnp.zeros((4, width), jnp.float32)]
    ).astype(bf16)
    full, full_hbm = shape_of(bf16, rows, width), in_hbm(bf16, rows, width)
    narrow_hbm = in_hbm(bf16, rows, width // 2)
    packed_rows = rows + mix.size // width
    (pack,) = in_place(
        pack_kernel, "pack", [inputs, mix], in_hbm(bf16, packed_rows, width), room=60
    )

    def block(k, packed, work=1):
        return in_place(
            block_kernel,
            f"block_{k}",
            [starts, packed, w_in],
            *([narrow_hbm] * 2 + [full_hbm]),
            *([narrow_hbm] * 2 if k == 2 else [full_hbm] * (1 + (k < 2))),
            work=work,
            scalars=1,
        )

    outer_pack, across_pack = hop(pack, INWARD), hop(pack, ACROSS)
    own = block(0, pack, 4 * rows * width * width)
    (d_hidden_own,) = in_place(
        d_hidden_kernel, "d_hidden", [w_out, grad_out], full, work=2 * rows * width * width
    )
    far_pack = hop(after(outer_pack, own[0], d_hidden_own), ACROSS)
    outer_cotan = hop(after(grad_out, outer_pack), INWARD)
    across_cotan = hop(after(grad_out, outer_pack), ACROSS)
    far_cotan = hop(outer_cotan, ACROSS)
    outer = block(1, after(outer_pack, coefs))
    across = block(3, after(across_pack, outer[0]))
    far = block(2, after(far_pack, outer_cotan, across[0]))

    blocks = [own, outer, far, across]
    gates = [part[2] for part in blocks]
    seg0 = [own[3], outer[3], across[3], far[3], far[4]]
    swapped = [hop(part, CORE_SWAP) for part in seg0]
    seg1, seg2, hidden, hidden_columns = kernel_call(
        forward_kernel,
        "forward_segments",
        room=60,
        grid=(rows // TILE,),
        in_specs=[scalar, whole(16, width)]
        + ([tile(width)] * 3 + [tile(width // 2)] * 2) * 2
        + [tile(width)] * 4,
        out_specs=[
            stacked(2, width),
            stacked(4, width),
            stacked(2, width),
            stacked(4, width // 2),
        ],
        out_shape=[
            shape_of(bf16, 2, rows, width),
            shape_of(bf16, 4, rows, width),
            shape_of(bf16, 2, rows, width),
            shape_of(bf16, 4, rows, width // 2),
        ],
        scratch_shapes=[pltpu.VMEM((4, TILE, width), bf16)],
    )(starts, coefs, *seg0, after(swapped[0], across_cotan), *swapped[1:], *gates)
    own_mixed, outer_mixed = in_place(
        mixed_kernel, "mixed", [hidden, w_out], full, full
    )
    sent_mixed = hop(outer_mixed, OUTWARD)

    d_hidden_outer, d_hidden_across = in_place(
        d_hidden_kernel,
        "d_hidden",
        [w_out, after(outer_cotan, outer_mixed), across_cotan],
        *[full] * 2,
    )
    (d_hidden_far,) = in_place(
        d_hidden_kernel, "d_hidden", [w_out, after(far_cotan, d_hidden_outer)], full
    )
    d_hidden = [d_hidden_own, d_hidden_outer, d_hidden_far, d_hidden_across]
    d_gate, *d_seg1, later_part = kernel_call(
        backward_kernel,
        "backward_segments",
        grid=(rows // TILE,),
        in_specs=[whole(16, width)]
        + [tile(width)] * 8
        + [stacked(2, width), stacked(4, width)],
        out_specs=[stacked(4, width)] + [tile(width)] * 4 + [whole(8, width)],
        out_shape=[shape_of(bf16, 4, rows, width)] + [full] * 4 + [shape_of(f32, 8, width)],
    )(coefs, *d_hidden, *gates, seg1, seg2)
    d_swapped = [hop(part, CORE_SWAP) for part in d_seg1]

    *early_given, early_kept = in_place(
        early_grads_kernel,
        "early_grads",
        [part[0] for part in blocks]
        + [d_gate, hidden_columns, grad_out, outer_cotan, far_cotan, across_cotan],
        *[shape_of(bf16, share, width)] * 4,
        shape_of(f32, 4 * share, width),
    )
    early_got = [hop(part, CORE_SWAP) for part in early_given]
    (early_sums,) = in_place(
        early_sums_kernel, "early_sums", [after(early_kept, sent_mixed, *d_swapped), *early_got], shape_of(bf16, 2 * share, width)
    )
    sent_early = hop(early_sums, OUTWARD)
    d_seg0, first_part = kernel_call(
        first_bit_kernel,
        "first_segment_grad",
        grid=(rows // TILE,),
        in_specs=[whole(16, width)] + [tile(width)] * 12,
        out_specs=[stacked(4, width), whole(8, width)],
        out_shape=[shape_of(bf16, 4, rows, width), shape_of(f32, 8, width)],
    )(coefs, *d_seg1, after(d_swapped[0], early_sums), *d_swapped[1:], *seg0[:2], *swapped[:2])
    own_d_acts, outer_d_acts = in_place(
        own_kernel,
        "own_grads",
        [d_seg0, d_gate, w_in, pack, outer_pack],
        full,
        full,
    )
    outer_handed = lax.ppermute(outer_d_acts, ("pipe", "seq"), relay_back(True))
    own_handed = lax.ppermute(own_d_acts, ("pipe", "seq"), relay_back(False))
    *late_given, late_here, late_there, own_square, outer_square = in_place(
        value_grads_kernel,
        "value_grads",
        [d_seg0, after(own[1], outer_d_acts)] + [part[1] for part in blocks[1:]] + [own[4], outer[4]],
        *[shape_of(bf16, share, width)] * 2,
        in_hbm(f32, share, width),
        shape_of(f32, share, width),
        in_hbm(f32, rows, rows),
        shape_of(f32, rows, rows),
    )
    late_got = [hop(part, CORE_SWAP) for part in late_given]
    (late_sums,) = in_place(
        late_sums_kernel,
        "late_sums",
        [after(late_there, sent_early), late_got[1], outer_square],
        shape_of(bf16, share + rows * rows // width, width),
    )
    sent_late = hop(late_sums, OUTWARD)
    def one_side(pair_terms, flip):
        empty = jnp.zeros_like(pair_terms)
        return jnp.where(
            flip == 1, jnp.stack([empty, pair_terms]), jnp.stack([pair_terms, empty])
        )

    first_terms, later_terms = lax.optimization_barrier(
        (first_part[:2], later_part, outer_d_acts, late_sums)
    )[:2]
    both = later_terms[:4].reshape(2, 2, width)
    terms = jnp.stack(
        [
            one_side(first_terms, flips[0]),
            jnp.where(flips[1] == 1, both[::-1], both),
            one_side(later_terms[4:6], flips[2]),
        ]
    )
    terms = terms + hop(terms, CORE_SWAP)
    terms = terms + hop(terms, ACROSS)
    twiddle_grad = jnp.where(inner, terms, hop(after(terms, sent_late), OUTWARD))

    mixed_out = jnp.where(inner, own_mixed, after(sent_mixed, sent_late))
    sent_early = after(sent_early, outer_d_acts)

    def share_of(kept, got, sent, at):
        mine = kept[2 * at * share : (2 * at + 1) * share] + wide(got[2 * at])
        return jnp.where(inner, mine, wide(sent[at * share : (at + 1) * share]))

    win_share = jnp.concatenate(
        [share_of(late_here, late_got, sent_late, 0), share_of(early_kept, early_got, sent_early, 0)],
        axis=1,
    )
    wout_share = share_of(early_kept, early_got, sent_early, 1)
    sent_square = jnp.concatenate(
        [sent_late[share:, i * rows : (i + 1) * rows] for i in range(width // rows)]
    )
    grad_square = jnp.where(inner, own_square, wide(sent_square))
    handed = jnp.where(inner, own_handed, outer_handed)
    return mixed_out, handed, win_share, wout_share, grad_square, twiddle_grad


def on_device(*arguments):
    plan = relay_plan if lax.axis_size("seq") == 8 else exchange_plan
    return tuple(result[None] for result in plan(*(part[0] for part in arguments)))


def solution(mesh):
    in_specs = (
        P("pipe", "seq", None),
        P("pipe", "seq", None),
        P("pipe", None, None),
        P("pipe", None, None),
        P("pipe", "seq", None),
        P("pipe", None, None, None, None),
    )
    out_specs = (
        P("pipe", "seq", None),
        P("pipe", "seq", None),
        P("pipe", "seq", None),
        P("pipe", "seq", None),
        P("pipe", "seq", None),
        P("pipe", None, None, None, None),
    )
    return jax.shard_map(
        on_device, mesh=mesh, in_specs=in_specs, out_specs=out_specs, check_vma=False
    )
```

```python
import functools

import jax
import jax.numpy as jnp
from jax import lax
from jax.experimental import pallas as pl
from jax.experimental.pallas import tpu as pltpu
from jax.sharding import PartitionSpec as P


def from_behind(value, axis, steps):
    count = lax.axis_size(axis)
    first, last = (max(0, -steps), min(count, count - steps))
    return lax.ppermute(value, axis, [(source, source + steps) for source in range(first, last)])


def local_segment(blocked, segment_coef, segment_bit):
    block_count, inner_rows, feature_count = blocked.shape
    stride_len = 2**segment_bit
    shaped = blocked.reshape(
        block_count // (2 * stride_len), 2, stride_len, inner_rows, feature_count
    )
    lower_part = shaped[:, 0].astype(jnp.float32)
    upper_part = shaped[:, 1].astype(jnp.float32)
    new_lower = segment_coef[0, 0] * lower_part + segment_coef[0, 1] * upper_part
    new_upper = segment_coef[1, 0] * upper_part + segment_coef[1, 1] * lower_part
    joined = jnp.stack([new_lower, new_upper], axis=1)
    return joined.reshape(block_count, inner_rows, feature_count).astype(jnp.bfloat16)


def local_back(grad_blocked, stored, segment_coef, segment_bit):
    block_count, inner_rows, feature_count = grad_blocked.shape
    stride_len = 2**segment_bit
    dshape = grad_blocked.reshape(
        block_count // (2 * stride_len), 2, stride_len, inner_rows, feature_count
    )
    zshape = stored.reshape(
        block_count // (2 * stride_len), 2, stride_len, inner_rows, feature_count
    )
    grad_lower = dshape[:, 0].astype(jnp.float32)
    grad_upper = dshape[:, 1].astype(jnp.float32)
    val_lower = zshape[:, 0].astype(jnp.float32)
    val_upper = zshape[:, 1].astype(jnp.float32)
    prev_lower = segment_coef[0, 0] * grad_lower + segment_coef[1, 1] * grad_upper
    prev_upper = segment_coef[1, 0] * grad_upper + segment_coef[0, 1] * grad_lower
    joined = jnp.stack([prev_lower, prev_upper], axis=1)
    prev = joined.reshape(block_count, inner_rows, feature_count).astype(jnp.bfloat16)
    axes_sum = (0, 1, 2)
    partial_value = jnp.stack(
        [
            jnp.stack(
                [
                    jnp.sum(grad_lower * val_lower, axis=axes_sum),
                    jnp.sum(grad_lower * val_upper, axis=axes_sum),
                ]
            ),
            jnp.stack(
                [
                    jnp.sum(grad_upper * val_upper, axis=axes_sum),
                    jnp.sum(grad_upper * val_lower, axis=axes_sum),
                ]
            ),
        ]
    )
    return (prev, partial_value)


def exchange_plan(inputs, grad_out, w_in, w_out, square_mix, twiddle_w):
    row_count, feature_count = inputs.shape
    seq_count = lax.axis_size("seq")
    segment_total = seq_count.bit_length() - 1
    projected = jnp.dot(inputs, w_in, preferred_element_type=jnp.float32)
    value = projected[:, :feature_count].astype(jnp.bfloat16)
    gate = projected[:, feature_count:].astype(jnp.bfloat16)
    first_segment = jnp.dot(square_mix, value, preferred_element_type=jnp.float32).astype(
        jnp.bfloat16
    )
    partials = [None] * segment_total
    columns = lax.all_to_all(first_segment, "seq", split_axis=0, concat_axis=0, tiled=True)
    blocked = columns.reshape(seq_count, row_count // seq_count, feature_count)
    stored = []
    for segment_bit in range(segment_total):
        stored.append(blocked)
        blocked = local_segment(blocked, twiddle_w[segment_bit], segment_bit)
    monarch = lax.all_to_all(
        blocked.reshape(row_count, feature_count), "seq", split_axis=0, concat_axis=0, tiled=True
    )
    hidden = (monarch.astype(jnp.float32) * gate.astype(jnp.float32)).astype(jnp.bfloat16)
    mixed_out = jnp.dot(hidden, w_out, preferred_element_type=jnp.float32).astype(jnp.bfloat16)
    d_hidden = lax.dot_general(
        grad_out, w_out, (((1,), (1,)), ((), ())), preferred_element_type=jnp.float32
    ).astype(jnp.bfloat16)
    wout_term = lax.dot_general(
        hidden, grad_out, (((0,), (0,)), ((), ())), preferred_element_type=jnp.float32
    )
    d_monarch = (d_hidden.astype(jnp.float32) * gate.astype(jnp.float32)).astype(jnp.bfloat16)
    d_gate = (d_hidden.astype(jnp.float32) * monarch.astype(jnp.float32)).astype(jnp.bfloat16)
    grad_columns = lax.all_to_all(d_monarch, "seq", split_axis=0, concat_axis=0, tiled=True)
    grad_blocked = grad_columns.reshape(seq_count, row_count // seq_count, feature_count)
    for segment_bit in range(segment_total - 1, -1, -1):
        grad_blocked, partials[segment_bit] = local_back(
            grad_blocked, stored[segment_bit], twiddle_w[segment_bit], segment_bit
        )
    d_first = lax.all_to_all(
        grad_blocked.reshape(row_count, feature_count),
        "seq",
        split_axis=0,
        concat_axis=0,
        tiled=True,
    )
    twiddle_grad = lax.psum(jnp.stack(partials), "seq")
    d_value = lax.dot_general(
        square_mix, d_first, (((0,), (0,)), ((), ())), preferred_element_type=jnp.float32
    ).astype(jnp.bfloat16)
    grad_square = lax.dot_general(
        d_first, value, (((1,), (1,)), ((), ())), preferred_element_type=jnp.float32
    )
    d_projected = jnp.concatenate([d_value, d_gate], axis=1)
    win_term = lax.dot_general(
        inputs, d_projected, (((0,), (0,)), ((), ())), preferred_element_type=jnp.float32
    )
    win_share, wout_share = (
        lax.psum_scatter(win_term, "seq", scatter_dimension=0, tiled=True),
        lax.psum_scatter(wout_term, "seq", scatter_dimension=0, tiled=True),
    )
    input_grad = lax.dot_general(
        d_projected, w_in, (((1,), (1,)), ((), ())), preferred_element_type=jnp.float32
    ).astype(jnp.bfloat16)
    handed = from_behind(input_grad, "pipe", -1)
    return mixed_out, handed, win_share, wout_share, grad_square, twiddle_grad


def chip_hops(hops):
    return [(2 * source + core, 2 * target + core) for source, target in hops for core in (0, 1)]


CORE_SWAP = [(index, index ^ 1) for index in range(8)]
INWARD = chip_hops([(0, 1), (3, 2)])
ACROSS = chip_hops([(1, 2), (2, 1)])
OUTWARD = chip_hops([(1, 0), (2, 3)])


def relay_back(outward):
    return [
        (8 * (section + 1) + source, 8 * section + target)
        for section in range(lax.axis_size("pipe") - 1)
        for source, target in (OUTWARD if outward else [(place, place) for place in range(2, 6)])
    ]


def hop(value, pairs):
    return lax.ppermute(value, "seq", pairs)


def dot(left, right):
    return jnp.dot(left, right, preferred_element_type=jnp.float32)


def dot_rows(left, right):
    return lax.dot_general(
        left, right, (((0,), (0,)), ((), ())), preferred_element_type=jnp.float32
    )


def dot_columns(left, right):
    return lax.dot_general(
        left, right, (((1,), (1,)), ((), ())), preferred_element_type=jnp.float32
    )


def narrow(value):
    return value.astype(jnp.bfloat16)


def wide(value):
    return value.astype(jnp.float32)


def coef_at(coef_ref, bit, side, term):
    return coef_ref[pl.ds(4 * bit + 2 * side + term, 1), :]


def cross(coef_ref, bit, side, own, other):
    return coef_at(coef_ref, bit, side, 0) * own + coef_at(coef_ref, bit, side, 1) * other


def cross_back(coef_ref, bit, side, own, other):
    return coef_at(coef_ref, bit, side, 0) * own + coef_at(coef_ref, bit, 1 - side, 1) * other


def pack_kernel(acts_ref, mix_ref, pack_ref):
    rows, width = acts_ref.shape
    depth = mix_ref.shape[1]
    piece = rows * depth // width
    pack_ref[pl.ds(0, rows), :] = acts_ref[...]
    for i in range(rows // piece):
        pack_ref[pl.ds(rows, piece), pl.ds(i * depth, depth)] = mix_ref[pl.ds(i * piece, piece), :]


def unpack_mix(pack_ref, rows):
    piece = pack_ref.shape[0] - rows
    return jnp.concatenate(
        [pack_ref[pl.ds(rows, piece), pl.ds(i * rows, rows)] for i in range(rows // piece)], axis=0
    )


def block_kernel(starts_ref, pack_ref, weight_ref, columns_ref, mixed_ref, gate_ref, *refs):
    rows, width = gate_ref.shape
    seg0, value = (refs[:2], ()) if refs[0].shape[1] < width else (refs[:1], refs[1:])
    half, share = width // 2, width // 8
    acts = pack_ref[pl.ds(0, rows), :]
    mix = unpack_mix(pack_ref, rows)
    for i in range(4):
        product = narrow(dot(acts, weight_ref[:, pl.ds(i * half, half)]))
        if i < 2:
            segment = narrow(dot(mix, product))
            if len(seg0) == 2:
                seg0[i][...] = segment
            else:
                seg0[0][:, pl.ds(i * half, half)] = segment
            if value:
                value[0][:, pl.ds(i * half, half)] = product
        else:
            gate_ref[:, pl.ds((i - 2) * half, half)] = product
    for j in range(4):
        start = pl.multiple_of(starts_ref[j], share)
        columns_ref[:, pl.ds(j * share, share)] = pack_ref[pl.ds(0, rows), pl.ds(start, share)]
    mixed_ref[...] = narrow(dot(mix, columns_ref[...]))


def d_hidden_kernel(weight_ref, *refs):
    for cotan_ref, out_ref in zip(refs[: len(refs) // 2], refs[len(refs) // 2 :]):
        out_ref[...] = narrow(dot_columns(cotan_ref[...], weight_ref[...]))


def early_grads_kernel(*refs):
    columns, d_gate_ref, hidden_ref, cotans = refs[0:4], refs[4], refs[5], refs[6:10]
    given_refs, kept_ref = refs[10:14], refs[14]
    half = kept_ref.shape[0] // 2
    d_gates = [d_gate_ref.at[k] for k in range(4)]
    split_grad(columns, d_gates, given_refs[0:2], [kept_ref.at[pl.ds(0, half), :]])
    hiddens = [hidden_ref.at[k] for k in range(4)]
    split_grad(hiddens, cotans, given_refs[2:4], [kept_ref.at[pl.ds(half, half), :]])


def split_grad(lefts, rights, given_refs, kept_refs):
    half = sum(ref.shape[0] for ref in kept_refs)
    for part in range(2):
        total = 0.0
        for left, right in zip(lefts, rights):
            total += dot_rows(left[:, pl.ds(part * half, half)], right[...])
        if part == 0:
            for i, ref in enumerate(given_refs):
                size = ref.shape[0]
                ref[...] = narrow(total[i * size : (i + 1) * size])
        else:
            for i, ref in enumerate(kept_refs):
                size = ref.shape[0]
                ref[...] = total[i * size : (i + 1) * size]


def value_grads_kernel(d_seg0_ref, *refs):
    values, given_refs, kept_refs = refs[4:6], refs[6:8], refs[8:10]
    split_grad(refs[0:4], [d_seg0_ref.at[k] for k in range(4)], given_refs, kept_refs)
    for k in range(2):
        refs[10 + k][...] = dot_columns(d_seg0_ref[k], values[k][...])


def early_sums_kernel(kept_ref, *refs):
    got, out_ref = refs[:4], refs[4]
    share = out_ref.shape[0] // 2
    for i in range(2):
        there = kept_ref[pl.ds((2 * i + 1) * share, share), :]
        out_ref[pl.ds(i * share, share), :] = narrow(there + wide(got[2 * i + 1][...]))


def late_sums_kernel(there_ref, got_ref, square_ref, out_ref):
    share = there_ref.shape[0]
    out_ref[pl.ds(0, share), :] = narrow(there_ref[...] + wide(got_ref[...]))
    depth = square_ref.shape[1]
    piece = out_ref.shape[0] - share
    for i in range(square_ref.shape[0] // piece):
        out_ref[pl.ds(share, piece), pl.ds(i * depth, depth)] = narrow(
            square_ref[pl.ds(i * piece, piece), :]
        )


def own_kernel(d_seg0_ref, d_gate_ref, weight_ref, *refs):
    packs, d_acts = refs[0:2], refs[2:4]
    rows, width = d_acts[0].shape
    for k in range(2):
        d_value = narrow(dot_rows(unpack_mix(packs[k], rows), d_seg0_ref[k]))
        d_acts[k][...] = narrow(
            dot_columns(d_value, weight_ref[:, pl.ds(0, width)])
            + dot_columns(d_gate_ref[k], weight_ref[:, pl.ds(width, width)])
        )


def mixed_kernel(hidden_ref, weight_ref, *outs):
    for k in range(2):
        outs[k][...] = narrow(dot(hidden_ref[k], weight_ref[...]))


def joined_far(refs):
    far = jnp.concatenate([refs[3][...], refs[4][...]], axis=1)
    return [refs[0][...], refs[1][...], far, refs[2][...]]


def forward_kernel(starts_ref, coef_ref, *refs):
    seg0, swapped = joined_far(refs[0:5]), joined_far(refs[5:10])
    gates = refs[10:14]
    seg1_out, seg2_out, hidden_out, columns_out, held = refs[14:19]
    share = coef_ref.shape[1] // 8
    first = [cross(coef_ref, 0, 0, seg0[k], swapped[k]) for k in range(4)]
    for k in range(2):
        seg1_out[k] = first[k]
    second = [cross(coef_ref, 1, k & 1, first[k], first[k ^ 1]) for k in range(4)]
    for k in range(4):
        seg2_out[k] = second[k]
    for k in range(4):
        hidden = cross(coef_ref, 2, k >> 1, second[k], second[k ^ 2]) * gates[k][...]
        held[k] = hidden
        if k < 2:
            hidden_out[k] = hidden
    for k in range(4):
        for j in range(4):
            start = pl.multiple_of(starts_ref[j], share)
            columns_out[k, :, pl.ds(j * share, share)] = held[k, :, pl.ds(start, share)]


def row_sums(value, row):
    shape = (8, value.shape[0])
    chosen = lax.broadcasted_iota(jnp.int32, shape, 0) == row
    return dot(jnp.where(chosen, 1.0, 0.0).astype(value.dtype), value)


def backward_kernel(coef_ref, *refs):
    d_hidden = refs[0:4]
    gates = refs[4:8]
    seg1_ref, seg2_ref = refs[8:10]
    d_gate_out, d_seg1_out, partial_out = refs[10], refs[11:15], refs[15]

    @pl.when(pl.program_id(0) == 0)
    def _():
        partial_out[...] = jnp.zeros_like(partial_out)

    third = []
    for k in range(4):
        grad = d_hidden[k][...]
        d_gate_out[k] = grad * cross(coef_ref, 2, k >> 1, seg2_ref[k], seg2_ref[k ^ 2])
        third.append(grad * gates[k][...])
    for k in range(2):
        partial_out[...] += row_sums(third[k] * seg2_ref[k], 4)
        partial_out[...] += row_sums(third[k] * seg2_ref[k ^ 2], 5)
    second = [cross_back(coef_ref, 2, k >> 1, third[k], third[k ^ 2]) for k in range(4)]
    for k in range(2):
        partial_out[...] += row_sums(second[k] * seg1_ref[k], 2 * k)
        partial_out[...] += row_sums(second[k] * seg1_ref[k ^ 1], 2 * k + 1)
    for k in range(4):
        d_seg1_out[k][...] = cross_back(coef_ref, 1, k & 1, second[k], second[k ^ 1])


def first_bit_kernel(coef_ref, *refs):
    d_seg1, d_swapped = refs[0:4], refs[4:8]
    seg0 = refs[8:10]
    swapped = refs[10:12]
    d_seg0_out, partial_out = refs[12:14]

    @pl.when(pl.program_id(0) == 0)
    def _():
        partial_out[...] = jnp.zeros_like(partial_out)

    for k in range(4):
        own, other = d_seg1[k][...], d_swapped[k][...]
        d_seg0 = cross_back(coef_ref, 0, 0, own, other)
        d_seg0_out[k] = d_seg0
        if k < 2:
            partial_out[...] += row_sums(own * seg0[k][...], 0)
            partial_out[...] += row_sums(own * swapped[k][...], 1)


TILE = 128


def tile(columns, column_at=0, row_at=0):
    return pl.BlockSpec((TILE, columns), lambda i: (i + row_at, column_at))


def stacked(count, columns, row_at=0):
    return pl.BlockSpec((count, TILE, columns), lambda i: (0, i + row_at, 0))


def whole(*shape):
    return pl.BlockSpec(shape, lambda i: (0,) * len(shape))


def shape_of(kind, *shape):
    return jax.ShapeDtypeStruct(shape, kind)


def in_hbm(kind, *shape):
    return pltpu.HBM(shape, kind)


def kernel_call(kernel, name, work=1, room=16, **settings):
    return pl.pallas_call(
        kernel,
        cost_estimate=pl.CostEstimate(flops=work, bytes_accessed=1, transcendentals=0),
        compiler_params=pltpu.CompilerParams(vmem_limit_bytes=room * 2**20),
        name=name,
        **settings,
    )


def in_place(kernel, name, operands, *outs, work=1, scalars=0, room=16):
    local = pl.BlockSpec(memory_space=pltpu.VMEM)
    return kernel_call(
        kernel,
        name,
        work,
        room,
        in_specs=[pl.BlockSpec(memory_space=pltpu.SMEM)] * scalars
        + [local] * (len(operands) - scalars),
        out_specs=[local] * len(outs),
        out_shape=list(outs),
    )(*operands)


def after(value, *earlier):
    return lax.optimization_barrier((value, *earlier))[0]


def relay_plan(inputs, grad_out, w_in, w_out, mix, twiddle_w):
    rows, width = inputs.shape
    share = width // 8
    bf16, f32 = jnp.bfloat16, jnp.float32
    place = lax.axis_index("seq")
    chip, core = place // 2, place % 2
    inner = (chip == 1) | (chip == 2)
    flips = (core, chip & 1, chip >> 1)
    scalar = pl.BlockSpec(memory_space=pltpu.SMEM)

    starts = jnp.stack(
        [
            (2 * (chip ^ chip_bit) + (core ^ core_bit)) * share
            for core_bit in (1, 0)
            for chip_bit in (0, 1)
        ]
    ).astype(jnp.int32)

    coefs = jnp.concatenate(
        [
            jnp.where(flips[bit] == 1, twiddle_w[bit][::-1], twiddle_w[bit]).reshape(4, width)
            for bit in range(3)
        ]
        + [jnp.zeros((4, width), jnp.float32)]
    ).astype(bf16)
    full, full_hbm = shape_of(bf16, rows, width), in_hbm(bf16, rows, width)
    narrow_hbm = in_hbm(bf16, rows, width // 2)
    packed_rows = rows + mix.size // width
    (pack,) = in_place(
        pack_kernel, "pack", [inputs, mix], in_hbm(bf16, packed_rows, width), room=60
    )

    def block(k, packed, work=1):
        return in_place(
            block_kernel,
            f"block_{k}",
            [starts, packed, w_in],
            *([narrow_hbm] * 2 + [full_hbm]),
            *([narrow_hbm] * 2 if k == 2 else [full_hbm] * (1 + (k < 2))),
            work=work,
            scalars=1,
        )

    outer_pack, across_pack = hop(pack, INWARD), hop(after(pack, coefs), ACROSS)
    own = block(0, pack, 4 * rows * width * width)
    (d_hidden_own,) = in_place(
        d_hidden_kernel, "d_hidden", [w_out, grad_out], full, work=2 * rows * width * width
    )
    far_pack = hop(after(outer_pack, own[0], d_hidden_own), ACROSS)
    outer_cotan = hop(after(grad_out, outer_pack), INWARD)
    across_cotan = hop(after(grad_out, outer_pack), ACROSS)
    outer = block(1, after(outer_pack, coefs))
    across = block(3, after(across_pack, outer[0]))
    far = block(2, after(far_pack, across[0]))
    far_cotan = hop(after(outer_cotan, far[0]), ACROSS)

    blocks = [own, outer, far, across]
    gates = [part[2] for part in blocks]
    seg0 = [own[3], outer[3], across[3], far[3], far[4]]
    swapped = [hop(part, CORE_SWAP) for part in seg0]
    seg1, seg2, hidden, hidden_columns = kernel_call(
        forward_kernel,
        "forward_segments",
        room=60,
        grid=(rows // TILE,),
        in_specs=[scalar, whole(16, width)]
        + ([tile(width)] * 3 + [tile(width // 2)] * 2) * 2
        + [tile(width)] * 4,
        out_specs=[
            stacked(2, width),
            stacked(4, width),
            stacked(2, width),
            stacked(4, width // 2),
        ],
        out_shape=[
            shape_of(bf16, 2, rows, width),
            shape_of(bf16, 4, rows, width),
            shape_of(bf16, 2, rows, width),
            shape_of(bf16, 4, rows, width // 2),
        ],
        scratch_shapes=[pltpu.VMEM((4, TILE, width), bf16)],
    )(starts, coefs, *seg0, *swapped, *gates)
    own_mixed, outer_mixed = in_place(
        mixed_kernel, "mixed", [after(hidden, across_cotan), w_out], full, full
    )
    sent_mixed = hop(outer_mixed, OUTWARD)

    d_hidden_outer, d_hidden_across = in_place(
        d_hidden_kernel,
        "d_hidden",
        [w_out, after(outer_cotan, outer_mixed), across_cotan],
        *[full] * 2,
    )
    (d_hidden_far,) = in_place(
        d_hidden_kernel, "d_hidden", [w_out, after(far_cotan, d_hidden_outer)], full
    )
    d_hidden = [d_hidden_own, d_hidden_outer, d_hidden_far, d_hidden_across]
    d_gate, *d_seg1, later_part = kernel_call(
        backward_kernel,
        "backward_segments",
        grid=(rows // TILE,),
        in_specs=[whole(16, width)]
        + [tile(width)] * 8
        + [stacked(2, width), stacked(4, width)],
        out_specs=[stacked(4, width)] + [tile(width)] * 4 + [whole(8, width)],
        out_shape=[shape_of(bf16, 4, rows, width)] + [full] * 4 + [shape_of(f32, 8, width)],
    )(coefs, *d_hidden, *gates, seg1, seg2)
    d_swapped = [hop(part, CORE_SWAP) for part in d_seg1]

    *early_given, early_kept = in_place(
        early_grads_kernel,
        "early_grads",
        [part[0] for part in blocks]
        + [d_gate, hidden_columns, grad_out, outer_cotan, far_cotan, across_cotan],
        *[shape_of(bf16, share, width)] * 4,
        shape_of(f32, 4 * share, width),
    )
    early_got = [hop(part, CORE_SWAP) for part in early_given]
    (early_sums,) = in_place(
        early_sums_kernel, "early_sums", [after(early_kept, sent_mixed, *d_swapped), *early_got], shape_of(bf16, 2 * share, width)
    )
    sent_early = hop(early_sums, OUTWARD)
    d_seg0, first_part = kernel_call(
        first_bit_kernel,
        "first_segment_grad",
        grid=(rows // TILE,),
        in_specs=[whole(16, width)] + [tile(width)] * 12,
        out_specs=[stacked(4, width), whole(8, width)],
        out_shape=[shape_of(bf16, 4, rows, width), shape_of(f32, 8, width)],
    )(coefs, *d_seg1, after(d_swapped[0], early_sums), *d_swapped[1:], *seg0[:2], *swapped[:2])
    own_d_acts, outer_d_acts = in_place(
        own_kernel,
        "own_grads",
        [d_seg0, d_gate, w_in, pack, outer_pack],
        full,
        full,
    )
    outer_handed = lax.ppermute(outer_d_acts, ("pipe", "seq"), relay_back(True))
    own_handed = lax.ppermute(own_d_acts, ("pipe", "seq"), relay_back(False))
    *late_given, late_here, late_there, own_square, outer_square = in_place(
        value_grads_kernel,
        "value_grads",
        [d_seg0, after(own[1], outer_d_acts)] + [part[1] for part in blocks[1:]] + [own[4], outer[4]],
        *[shape_of(bf16, share, width)] * 2,
        in_hbm(f32, share, width),
        shape_of(f32, share, width),
        in_hbm(f32, rows, rows),
        shape_of(f32, rows, rows),
    )
    late_got = [hop(part, CORE_SWAP) for part in late_given]
    (late_sums,) = in_place(
        late_sums_kernel,
        "late_sums",
        [after(late_there, sent_early), late_got[1], outer_square],
        shape_of(bf16, share + rows * rows // width, width),
    )
    sent_late = hop(late_sums, OUTWARD)
    def one_side(pair_terms, flip):
        empty = jnp.zeros_like(pair_terms)
        return jnp.where(
            flip == 1, jnp.stack([empty, pair_terms]), jnp.stack([pair_terms, empty])
        )

    first_terms, later_terms = lax.optimization_barrier(
        (first_part[:2], later_part, outer_d_acts, late_sums)
    )[:2]
    both = later_terms[:4].reshape(2, 2, width)
    terms = jnp.stack(
        [
            one_side(first_terms, flips[0]),
            jnp.where(flips[1] == 1, both[::-1], both),
            one_side(later_terms[4:6], flips[2]),
        ]
    )
    terms = terms + hop(terms, CORE_SWAP)
    terms = after(terms, outer_handed)
    terms = terms + hop(terms, ACROSS)
    twiddle_grad = jnp.where(inner, terms, hop(after(terms, late_sums), OUTWARD))

    mixed_out = jnp.where(inner, own_mixed, after(sent_mixed, sent_late))
    sent_early = after(sent_early, outer_d_acts)

    def share_of(kept, got, sent, at):
        mine = kept[2 * at * share : (2 * at + 1) * share] + wide(got[2 * at])
        return jnp.where(inner, mine, wide(sent[at * share : (at + 1) * share]))

    win_share = jnp.concatenate(
        [share_of(late_here, late_got, sent_late, 0), share_of(early_kept, early_got, sent_early, 0)],
        axis=1,
    )
    wout_share = share_of(early_kept, early_got, sent_early, 1)
    sent_square = jnp.concatenate(
        [sent_late[share:, i * rows : (i + 1) * rows] for i in range(width // rows)]
    )
    grad_square = jnp.where(inner, own_square, wide(sent_square))
    handed = jnp.where(inner, own_handed, outer_handed)
    return mixed_out, handed, win_share, wout_share, grad_square, twiddle_grad


def on_device(*arguments):
    plan = relay_plan if lax.axis_size("seq") == 8 else exchange_plan
    return tuple(result[None] for result in plan(*(part[0] for part in arguments)))


def solution(mesh):
    in_specs = (
        P("pipe", "seq", None),
        P("pipe", "seq", None),
        P("pipe", None, None),
        P("pipe", None, None),
        P("pipe", "seq", None),
        P("pipe", None, None, None, None),
    )
    out_specs = (
        P("pipe", "seq", None),
        P("pipe", "seq", None),
        P("pipe", "seq", None),
        P("pipe", "seq", None),
        P("pipe", "seq", None),
        P("pipe", None, None, None, None),
    )
    return jax.shard_map(
        on_device, mesh=mesh, in_specs=in_specs, out_specs=out_specs, check_vma=False
    )
```

```python
import functools

import jax
import jax.numpy as jnp
from jax import lax
from jax.experimental import pallas as pl
from jax.experimental.pallas import tpu as pltpu
from jax.sharding import PartitionSpec as P


def from_behind(value, axis, steps):
    count = lax.axis_size(axis)
    first, last = (max(0, -steps), min(count, count - steps))
    return lax.ppermute(value, axis, [(source, source + steps) for source in range(first, last)])


def local_segment(blocked, segment_coef, segment_bit):
    block_count, inner_rows, feature_count = blocked.shape
    stride_len = 2**segment_bit
    shaped = blocked.reshape(
        block_count // (2 * stride_len), 2, stride_len, inner_rows, feature_count
    )
    lower_part = shaped[:, 0].astype(jnp.float32)
    upper_part = shaped[:, 1].astype(jnp.float32)
    new_lower = segment_coef[0, 0] * lower_part + segment_coef[0, 1] * upper_part
    new_upper = segment_coef[1, 0] * upper_part + segment_coef[1, 1] * lower_part
    joined = jnp.stack([new_lower, new_upper], axis=1)
    return joined.reshape(block_count, inner_rows, feature_count).astype(jnp.bfloat16)


def local_back(grad_blocked, stored, segment_coef, segment_bit):
    block_count, inner_rows, feature_count = grad_blocked.shape
    stride_len = 2**segment_bit
    dshape = grad_blocked.reshape(
        block_count // (2 * stride_len), 2, stride_len, inner_rows, feature_count
    )
    zshape = stored.reshape(
        block_count // (2 * stride_len), 2, stride_len, inner_rows, feature_count
    )
    grad_lower = dshape[:, 0].astype(jnp.float32)
    grad_upper = dshape[:, 1].astype(jnp.float32)
    val_lower = zshape[:, 0].astype(jnp.float32)
    val_upper = zshape[:, 1].astype(jnp.float32)
    prev_lower = segment_coef[0, 0] * grad_lower + segment_coef[1, 1] * grad_upper
    prev_upper = segment_coef[1, 0] * grad_upper + segment_coef[0, 1] * grad_lower
    joined = jnp.stack([prev_lower, prev_upper], axis=1)
    prev = joined.reshape(block_count, inner_rows, feature_count).astype(jnp.bfloat16)
    axes_sum = (0, 1, 2)
    partial_value = jnp.stack(
        [
            jnp.stack(
                [
                    jnp.sum(grad_lower * val_lower, axis=axes_sum),
                    jnp.sum(grad_lower * val_upper, axis=axes_sum),
                ]
            ),
            jnp.stack(
                [
                    jnp.sum(grad_upper * val_upper, axis=axes_sum),
                    jnp.sum(grad_upper * val_lower, axis=axes_sum),
                ]
            ),
        ]
    )
    return (prev, partial_value)


def exchange_plan(inputs, grad_out, w_in, w_out, square_mix, twiddle_w):
    row_count, feature_count = inputs.shape
    seq_count = lax.axis_size("seq")
    segment_total = seq_count.bit_length() - 1
    projected = jnp.dot(inputs, w_in, preferred_element_type=jnp.float32)
    value = projected[:, :feature_count].astype(jnp.bfloat16)
    gate = projected[:, feature_count:].astype(jnp.bfloat16)
    first_segment = jnp.dot(square_mix, value, preferred_element_type=jnp.float32).astype(
        jnp.bfloat16
    )
    partials = [None] * segment_total
    columns = lax.all_to_all(first_segment, "seq", split_axis=0, concat_axis=0, tiled=True)
    blocked = columns.reshape(seq_count, row_count // seq_count, feature_count)
    stored = []
    for segment_bit in range(segment_total):
        stored.append(blocked)
        blocked = local_segment(blocked, twiddle_w[segment_bit], segment_bit)
    monarch = lax.all_to_all(
        blocked.reshape(row_count, feature_count), "seq", split_axis=0, concat_axis=0, tiled=True
    )
    hidden = (monarch.astype(jnp.float32) * gate.astype(jnp.float32)).astype(jnp.bfloat16)
    mixed_out = jnp.dot(hidden, w_out, preferred_element_type=jnp.float32).astype(jnp.bfloat16)
    d_hidden = lax.dot_general(
        grad_out, w_out, (((1,), (1,)), ((), ())), preferred_element_type=jnp.float32
    ).astype(jnp.bfloat16)
    wout_term = lax.dot_general(
        hidden, grad_out, (((0,), (0,)), ((), ())), preferred_element_type=jnp.float32
    )
    d_monarch = (d_hidden.astype(jnp.float32) * gate.astype(jnp.float32)).astype(jnp.bfloat16)
    d_gate = (d_hidden.astype(jnp.float32) * monarch.astype(jnp.float32)).astype(jnp.bfloat16)
    grad_columns = lax.all_to_all(d_monarch, "seq", split_axis=0, concat_axis=0, tiled=True)
    grad_blocked = grad_columns.reshape(seq_count, row_count // seq_count, feature_count)
    for segment_bit in range(segment_total - 1, -1, -1):
        grad_blocked, partials[segment_bit] = local_back(
            grad_blocked, stored[segment_bit], twiddle_w[segment_bit], segment_bit
        )
    d_first = lax.all_to_all(
        grad_blocked.reshape(row_count, feature_count),
        "seq",
        split_axis=0,
        concat_axis=0,
        tiled=True,
    )
    twiddle_grad = lax.psum(jnp.stack(partials), "seq")
    d_value = lax.dot_general(
        square_mix, d_first, (((0,), (0,)), ((), ())), preferred_element_type=jnp.float32
    ).astype(jnp.bfloat16)
    grad_square = lax.dot_general(
        d_first, value, (((1,), (1,)), ((), ())), preferred_element_type=jnp.float32
    )
    d_projected = jnp.concatenate([d_value, d_gate], axis=1)
    win_term = lax.dot_general(
        inputs, d_projected, (((0,), (0,)), ((), ())), preferred_element_type=jnp.float32
    )
    win_share, wout_share = (
        lax.psum_scatter(win_term, "seq", scatter_dimension=0, tiled=True),
        lax.psum_scatter(wout_term, "seq", scatter_dimension=0, tiled=True),
    )
    input_grad = lax.dot_general(
        d_projected, w_in, (((1,), (1,)), ((), ())), preferred_element_type=jnp.float32
    ).astype(jnp.bfloat16)
    handed = from_behind(input_grad, "pipe", -1)
    return mixed_out, handed, win_share, wout_share, grad_square, twiddle_grad


def chip_hops(hops):
    return [(2 * source + core, 2 * target + core) for source, target in hops for core in (0, 1)]


CORE_SWAP = [(index, index ^ 1) for index in range(8)]
INWARD = chip_hops([(0, 1), (3, 2)])
ACROSS = chip_hops([(1, 2), (2, 1)])
OUTWARD = chip_hops([(1, 0), (2, 3)])


def relay_back(outward):
    return [
        (8 * (section + 1) + source, 8 * section + target)
        for section in range(lax.axis_size("pipe") - 1)
        for source, target in (OUTWARD if outward else [(place, place) for place in range(2, 6)])
    ]


def hop(value, pairs):
    return lax.ppermute(value, "seq", pairs)


def dot(left, right):
    return jnp.dot(left, right, preferred_element_type=jnp.float32)


def dot_rows(left, right):
    return lax.dot_general(
        left, right, (((0,), (0,)), ((), ())), preferred_element_type=jnp.float32
    )


def dot_columns(left, right):
    return lax.dot_general(
        left, right, (((1,), (1,)), ((), ())), preferred_element_type=jnp.float32
    )


def narrow(value):
    return value.astype(jnp.bfloat16)


def wide(value):
    return value.astype(jnp.float32)


def coef_at(coef_ref, bit, side, term):
    return coef_ref[pl.ds(4 * bit + 2 * side + term, 1), :]


def cross(coef_ref, bit, side, own, other):
    return coef_at(coef_ref, bit, side, 0) * own + coef_at(coef_ref, bit, side, 1) * other


def cross_back(coef_ref, bit, side, own, other):
    return coef_at(coef_ref, bit, side, 0) * own + coef_at(coef_ref, bit, 1 - side, 1) * other


def pack_kernel(acts_ref, mix_ref, pack_ref):
    rows, width = acts_ref.shape
    depth = mix_ref.shape[1]
    piece = rows * depth // width
    pack_ref[pl.ds(0, rows), :] = acts_ref[...]
    for i in range(rows // piece):
        pack_ref[pl.ds(rows, piece), pl.ds(i * depth, depth)] = mix_ref[pl.ds(i * piece, piece), :]


def unpack_mix(pack_ref, rows):
    piece = pack_ref.shape[0] - rows
    return jnp.concatenate(
        [pack_ref[pl.ds(rows, piece), pl.ds(i * rows, rows)] for i in range(rows // piece)], axis=0
    )


def block_kernel(starts_ref, pack_ref, weight_ref, columns_ref, mixed_ref, gate_ref, *refs):
    rows, width = gate_ref.shape
    seg0, value = (refs[:2], ()) if refs[0].shape[1] < width else (refs[:1], refs[1:])
    half, share = width // 2, width // 8
    acts = pack_ref[pl.ds(0, rows), :]
    mix = unpack_mix(pack_ref, rows)
    for i in range(4):
        product = narrow(dot(acts, weight_ref[:, pl.ds(i * half, half)]))
        if i < 2:
            segment = narrow(dot(mix, product))
            if len(seg0) == 2:
                seg0[i][...] = segment
            else:
                seg0[0][:, pl.ds(i * half, half)] = segment
            if value:
                value[0][:, pl.ds(i * half, half)] = product
        else:
            gate_ref[:, pl.ds((i - 2) * half, half)] = product
    for j in range(4):
        start = pl.multiple_of(starts_ref[j], share)
        columns_ref[:, pl.ds(j * share, share)] = pack_ref[pl.ds(0, rows), pl.ds(start, share)]
    mixed_ref[...] = narrow(dot(mix, columns_ref[...]))


def d_hidden_kernel(weight_ref, *refs):
    for cotan_ref, out_ref in zip(refs[: len(refs) // 2], refs[len(refs) // 2 :]):
        out_ref[...] = narrow(dot_columns(cotan_ref[...], weight_ref[...]))


def early_grads_kernel(*refs):
    columns, d_gate_ref, hidden_ref, cotans = refs[0:4], refs[4], refs[5], refs[6:10]
    given_refs, kept_ref = refs[10:14], refs[14]
    half = kept_ref.shape[0] // 2
    d_gates = [d_gate_ref.at[k] for k in range(4)]
    split_grad(columns, d_gates, given_refs[0:2], [kept_ref.at[pl.ds(0, half), :]])
    hiddens = [hidden_ref.at[k] for k in range(4)]
    split_grad(hiddens, cotans, given_refs[2:4], [kept_ref.at[pl.ds(half, half), :]])


def split_grad(lefts, rights, given_refs, kept_refs):
    half = sum(ref.shape[0] for ref in kept_refs)
    for part in range(2):
        total = 0.0
        for left, right in zip(lefts, rights):
            total += dot_rows(left[:, pl.ds(part * half, half)], right[...])
        if part == 0:
            for i, ref in enumerate(given_refs):
                size = ref.shape[0]
                ref[...] = narrow(total[i * size : (i + 1) * size])
        else:
            for i, ref in enumerate(kept_refs):
                size = ref.shape[0]
                ref[...] = total[i * size : (i + 1) * size]


def value_grads_kernel(d_seg0_ref, *refs):
    values, given_refs, kept_refs = refs[4:6], refs[6:8], refs[8:10]
    split_grad(refs[0:4], [d_seg0_ref.at[k] for k in range(4)], given_refs, kept_refs)
    for k in range(2):
        refs[10 + k][...] = dot_columns(d_seg0_ref[k], values[k][...])


def early_sums_kernel(kept_ref, *refs):
    got, out_ref = refs[:4], refs[4]
    share = out_ref.shape[0] // 2
    for i in range(2):
        there = kept_ref[pl.ds((2 * i + 1) * share, share), :]
        out_ref[pl.ds(i * share, share), :] = narrow(there + wide(got[2 * i + 1][...]))


def late_sums_kernel(there_ref, got_ref, square_ref, out_ref):
    share = there_ref.shape[0]
    out_ref[pl.ds(0, share), :] = narrow(there_ref[...] + wide(got_ref[...]))
    depth = square_ref.shape[1]
    piece = out_ref.shape[0] - share
    for i in range(square_ref.shape[0] // piece):
        out_ref[pl.ds(share, piece), pl.ds(i * depth, depth)] = narrow(
            square_ref[pl.ds(i * piece, piece), :]
        )


def own_kernel(d_seg0_ref, d_gate_ref, weight_ref, *refs):
    packs, d_acts = refs[0:2], refs[2:4]
    rows, width = d_acts[0].shape
    for k in range(2):
        d_value = narrow(dot_rows(unpack_mix(packs[k], rows), d_seg0_ref[k]))
        d_acts[k][...] = narrow(
            dot_columns(d_value, weight_ref[:, pl.ds(0, width)])
            + dot_columns(d_gate_ref[k], weight_ref[:, pl.ds(width, width)])
        )


def mixed_kernel(hidden_ref, weight_ref, *outs):
    for k in range(2):
        outs[k][...] = narrow(dot(hidden_ref[k], weight_ref[...]))


def joined_far(refs):
    far = jnp.concatenate([refs[3][...], refs[4][...]], axis=1)
    return [refs[0][...], refs[1][...], far, refs[2][...]]


def forward_kernel(starts_ref, coef_ref, *refs):
    seg0, swapped = joined_far(refs[0:5]), joined_far(refs[5:10])
    gates = refs[10:14]
    seg1_out, seg2_out, hidden_out, columns_out, held = refs[14:19]
    share = coef_ref.shape[1] // 8
    first = [cross(coef_ref, 0, 0, seg0[k], swapped[k]) for k in range(4)]
    for k in range(2):
        seg1_out[k] = first[k]
    second = [cross(coef_ref, 1, k & 1, first[k], first[k ^ 1]) for k in range(4)]
    for k in range(4):
        seg2_out[k] = second[k]
    for k in range(4):
        hidden = cross(coef_ref, 2, k >> 1, second[k], second[k ^ 2]) * gates[k][...]
        held[k] = hidden
        if k < 2:
            hidden_out[k] = hidden
    for k in range(4):
        for j in range(4):
            start = pl.multiple_of(starts_ref[j], share)
            columns_out[k, :, pl.ds(j * share, share)] = held[k, :, pl.ds(start, share)]


def row_sums(value, row):
    shape = (8, value.shape[0])
    chosen = lax.broadcasted_iota(jnp.int32, shape, 0) == row
    return dot(jnp.where(chosen, 1.0, 0.0).astype(value.dtype), value)


def backward_kernel(coef_ref, *refs):
    d_hidden = refs[0:4]
    gates = refs[4:8]
    seg1_ref, seg2_ref = refs[8:10]
    d_gate_out, d_seg1_out, partial_out = refs[10], refs[11:15], refs[15]

    @pl.when(pl.program_id(0) == 0)
    def _():
        partial_out[...] = jnp.zeros_like(partial_out)

    third = []
    for k in range(4):
        grad = d_hidden[k][...]
        d_gate_out[k] = grad * cross(coef_ref, 2, k >> 1, seg2_ref[k], seg2_ref[k ^ 2])
        third.append(grad * gates[k][...])
    for k in range(2):
        partial_out[...] += row_sums(third[k] * seg2_ref[k], 4)
        partial_out[...] += row_sums(third[k] * seg2_ref[k ^ 2], 5)
    second = [cross_back(coef_ref, 2, k >> 1, third[k], third[k ^ 2]) for k in range(4)]
    for k in range(2):
        partial_out[...] += row_sums(second[k] * seg1_ref[k], 2 * k)
        partial_out[...] += row_sums(second[k] * seg1_ref[k ^ 1], 2 * k + 1)
    for k in range(4):
        d_seg1_out[k][...] = cross_back(coef_ref, 1, k & 1, second[k], second[k ^ 1])


def first_bit_kernel(coef_ref, *refs):
    d_seg1, d_swapped = refs[0:4], refs[4:8]
    seg0 = refs[8:10]
    swapped = refs[10:12]
    d_seg0_out, partial_out = refs[12:14]

    @pl.when(pl.program_id(0) == 0)
    def _():
        partial_out[...] = jnp.zeros_like(partial_out)

    for k in range(4):
        own, other = d_seg1[k][...], d_swapped[k][...]
        d_seg0 = cross_back(coef_ref, 0, 0, own, other)
        d_seg0_out[k] = d_seg0
        if k < 2:
            partial_out[...] += row_sums(own * seg0[k][...], 0)
            partial_out[...] += row_sums(own * swapped[k][...], 1)


TILE = 128


def tile(columns, column_at=0, row_at=0):
    return pl.BlockSpec((TILE, columns), lambda i: (i + row_at, column_at))


def stacked(count, columns, row_at=0):
    return pl.BlockSpec((count, TILE, columns), lambda i: (0, i + row_at, 0))


def whole(*shape):
    return pl.BlockSpec(shape, lambda i: (0,) * len(shape))


def shape_of(kind, *shape):
    return jax.ShapeDtypeStruct(shape, kind)


def in_hbm(kind, *shape):
    return pltpu.HBM(shape, kind)


def kernel_call(kernel, name, work=1, room=16, **settings):
    return pl.pallas_call(
        kernel,
        cost_estimate=pl.CostEstimate(flops=work, bytes_accessed=1, transcendentals=0),
        compiler_params=pltpu.CompilerParams(vmem_limit_bytes=room * 2**20),
        name=name,
        **settings,
    )


def in_place(kernel, name, operands, *outs, work=1, scalars=0, room=16):
    local = pl.BlockSpec(memory_space=pltpu.VMEM)
    return kernel_call(
        kernel,
        name,
        work,
        room,
        in_specs=[pl.BlockSpec(memory_space=pltpu.SMEM)] * scalars
        + [local] * (len(operands) - scalars),
        out_specs=[local] * len(outs),
        out_shape=list(outs),
    )(*operands)


def after(value, *earlier):
    return lax.optimization_barrier((value, *earlier))[0]


def relay_plan(inputs, grad_out, w_in, w_out, mix, twiddle_w):
    rows, width = inputs.shape
    share = width // 8
    bf16, f32 = jnp.bfloat16, jnp.float32
    place = lax.axis_index("seq")
    chip, core = place // 2, place % 2
    inner = (chip == 1) | (chip == 2)
    flips = (core, chip & 1, chip >> 1)
    scalar = pl.BlockSpec(memory_space=pltpu.SMEM)

    starts = jnp.stack(
        [
            (2 * (chip ^ chip_bit) + (core ^ core_bit)) * share
            for core_bit in (1, 0)
            for chip_bit in (0, 1)
        ]
    ).astype(jnp.int32)

    coefs = jnp.concatenate(
        [
            jnp.where(flips[bit] == 1, twiddle_w[bit][::-1], twiddle_w[bit]).reshape(4, width)
            for bit in range(3)
        ]
        + [jnp.zeros((4, width), jnp.float32)]
    ).astype(bf16)
    full, full_hbm = shape_of(bf16, rows, width), in_hbm(bf16, rows, width)
    narrow_hbm = in_hbm(bf16, rows, width // 2)
    packed_rows = rows + mix.size // width
    (pack,) = in_place(
        pack_kernel, "pack", [inputs, mix], in_hbm(bf16, packed_rows, width), room=60
    )

    def block(k, packed, work=1):
        return in_place(
            block_kernel,
            f"block_{k}",
            [starts, packed, w_in],
            *([narrow_hbm] * 2 + [full_hbm]),
            *([narrow_hbm] * 2 if k == 2 else [full_hbm] * (1 + (k < 2))),
            work=work,
            scalars=1,
        )

    outer_pack, across_pack = hop(pack, INWARD), hop(after(pack, coefs), ACROSS)
    own = block(0, pack, 4 * rows * width * width)
    (d_hidden_own,) = in_place(
        d_hidden_kernel, "d_hidden", [w_out, grad_out], full, work=2 * rows * width * width
    )
    far_pack = hop(after(outer_pack, own[0], d_hidden_own), ACROSS)
    outer_cotan = hop(after(grad_out, outer_pack), INWARD)
    across_cotan = hop(after(grad_out, outer_pack), ACROSS)
    outer = block(1, after(outer_pack, coefs))
    across = block(3, after(across_pack, outer[0]))
    far = block(2, after(far_pack, across[0]))
    far_cotan = hop(after(outer_cotan, far[0]), ACROSS)

    blocks = [own, outer, far, across]
    gates = [part[2] for part in blocks]
    seg0 = [own[3], outer[3], across[3], far[3], far[4]]
    swapped = [hop(part, CORE_SWAP) for part in seg0]
    seg1, seg2, hidden, hidden_columns = kernel_call(
        forward_kernel,
        "forward_segments",
        room=60,
        grid=(rows // TILE,),
        in_specs=[scalar, whole(16, width)]
        + ([tile(width)] * 3 + [tile(width // 2)] * 2) * 2
        + [tile(width)] * 4,
        out_specs=[
            stacked(2, width),
            stacked(4, width),
            stacked(2, width),
            stacked(4, width // 2),
        ],
        out_shape=[
            shape_of(bf16, 2, rows, width),
            shape_of(bf16, 4, rows, width),
            shape_of(bf16, 2, rows, width),
            shape_of(bf16, 4, rows, width // 2),
        ],
        scratch_shapes=[pltpu.VMEM((4, TILE, width), bf16)],
    )(starts, coefs, *seg0, *swapped, *gates)
    own_mixed, outer_mixed = in_place(
        mixed_kernel, "mixed", [after(hidden, across_cotan), w_out], full, full
    )
    sent_mixed = hop(outer_mixed, OUTWARD)

    d_hidden_outer, d_hidden_across = in_place(
        d_hidden_kernel,
        "d_hidden",
        [w_out, after(outer_cotan, outer_mixed), across_cotan],
        *[full] * 2,
    )
    (d_hidden_far,) = in_place(
        d_hidden_kernel, "d_hidden", [w_out, after(far_cotan, d_hidden_outer)], full
    )
    d_hidden = [d_hidden_own, d_hidden_outer, d_hidden_far, d_hidden_across]
    d_gate, *d_seg1, later_part = kernel_call(
        backward_kernel,
        "backward_segments",
        grid=(rows // TILE,),
        in_specs=[whole(16, width)]
        + [tile(width)] * 8
        + [stacked(2, width), stacked(4, width)],
        out_specs=[stacked(4, width)] + [tile(width)] * 4 + [whole(8, width)],
        out_shape=[shape_of(bf16, 4, rows, width)] + [full] * 4 + [shape_of(f32, 8, width)],
    )(coefs, *d_hidden, *gates, seg1, seg2)
    d_swapped = [hop(part, CORE_SWAP) for part in d_seg1]

    *early_given, early_kept = in_place(
        early_grads_kernel,
        "early_grads",
        [part[0] for part in blocks]
        + [d_gate, hidden_columns, grad_out, outer_cotan, far_cotan, across_cotan],
        *[shape_of(bf16, share, width)] * 4,
        shape_of(f32, 4 * share, width),
    )
    early_got = [hop(part, CORE_SWAP) for part in early_given]
    (early_sums,) = in_place(
        early_sums_kernel, "early_sums", [after(early_kept, sent_mixed, *d_swapped), *early_got], shape_of(bf16, 2 * share, width)
    )
    sent_early = hop(early_sums, OUTWARD)
    d_seg0, first_part = kernel_call(
        first_bit_kernel,
        "first_segment_grad",
        grid=(rows // TILE,),
        in_specs=[whole(16, width)] + [tile(width)] * 12,
        out_specs=[stacked(4, width), whole(8, width)],
        out_shape=[shape_of(bf16, 4, rows, width), shape_of(f32, 8, width)],
    )(coefs, *d_seg1, after(d_swapped[0], early_sums), *d_swapped[1:], *seg0[:2], *swapped[:2])
    own_d_acts, outer_d_acts = in_place(
        own_kernel,
        "own_grads",
        [d_seg0, d_gate, w_in, pack, outer_pack],
        full,
        full,
    )
    outer_handed = lax.ppermute(outer_d_acts, ("pipe", "seq"), relay_back(True))
    own_handed = lax.ppermute(own_d_acts, ("pipe", "seq"), relay_back(False))
    *late_given, late_here, late_there, own_square, outer_square = in_place(
        value_grads_kernel,
        "value_grads",
        [d_seg0, after(own[1], outer_d_acts)] + [part[1] for part in blocks[1:]] + [own[4], outer[4]],
        *[shape_of(bf16, share, width)] * 2,
        in_hbm(f32, share, width),
        shape_of(f32, share, width),
        in_hbm(f32, rows, rows),
        shape_of(f32, rows, rows),
    )
    late_got = [hop(part, CORE_SWAP) for part in late_given]
    (late_sums,) = in_place(
        late_sums_kernel,
        "late_sums",
        [after(late_there, sent_early), late_got[1], outer_square],
        shape_of(bf16, share + rows * rows // width, width),
    )
    sent_late = hop(late_sums, OUTWARD)
    def one_side(pair_terms, flip):
        empty = jnp.zeros_like(pair_terms)
        return jnp.where(
            flip == 1, jnp.stack([empty, pair_terms]), jnp.stack([pair_terms, empty])
        )

    first_terms, later_terms = lax.optimization_barrier(
        (first_part[:2], later_part, outer_d_acts, late_sums)
    )[:2]
    both = later_terms[:4].reshape(2, 2, width)
    terms = jnp.stack(
        [
            one_side(first_terms, flips[0]),
            jnp.where(flips[1] == 1, both[::-1], both),
            one_side(later_terms[4:6], flips[2]),
        ]
    )
    terms = terms + hop(terms, CORE_SWAP)
    terms = terms + hop(terms, ACROSS)
    sent_terms = hop(after(terms, late_sums), OUTWARD)

    mixed_out = jnp.where(inner, own_mixed, after(sent_mixed, sent_late))
    sent_early = after(sent_early, outer_d_acts)

    def share_of(kept, got, sent, at):
        mine = kept[2 * at * share : (2 * at + 1) * share] + wide(got[2 * at])
        return jnp.where(inner, mine, wide(sent[at * share : (at + 1) * share]))

    win_share = jnp.concatenate(
        [share_of(late_here, late_got, sent_late, 0), share_of(early_kept, early_got, sent_early, 0)],
        axis=1,
    )
    wout_share = share_of(early_kept, early_got, sent_early, 1)
    sent_square = jnp.concatenate(
        [sent_late[share:, i * rows : (i + 1) * rows] for i in range(width // rows)]
    )
    grad_square = jnp.where(inner, own_square, wide(sent_square))
    handed = jnp.where(inner, own_handed, outer_handed)
    sent_terms = after(sent_terms, win_share, wout_share, grad_square, mixed_out, handed)
    twiddle_grad = jnp.where(inner, terms, sent_terms)
    return mixed_out, handed, win_share, wout_share, grad_square, twiddle_grad


def on_device(*arguments):
    plan = relay_plan if lax.axis_size("seq") == 8 else exchange_plan
    return tuple(result[None] for result in plan(*(part[0] for part in arguments)))


def solution(mesh):
    in_specs = (
        P("pipe", "seq", None),
        P("pipe", "seq", None),
        P("pipe", None, None),
        P("pipe", None, None),
        P("pipe", "seq", None),
        P("pipe", None, None, None, None),
    )
    out_specs = (
        P("pipe", "seq", None),
        P("pipe", "seq", None),
        P("pipe", "seq", None),
        P("pipe", "seq", None),
        P("pipe", "seq", None),
        P("pipe", None, None, None, None),
    )
    return jax.shard_map(
        on_device, mesh=mesh, in_specs=in_specs, out_specs=out_specs, check_vma=False
    )
```
